128 devices in a mesh: gx: 16 (over y, x), gy: 8 (over z, core).
Axes of the slice: x: 4, y: 4, z: 4, core: 2. Of those that a mesh axis runs over, the one named last changes fastest.
Arguments:
- composition: float32 [53, 1048576], P(None, ('gx', 'gy')), may hold values from -6 to 6
- particle_mass: float32 [1048576], P(('gx', 'gy')), may hold values from 0.3 to 3
- particle_cell: int32 [2, 1048576], P(None, ('gx', 'gy')), may hold values from 0 to 1023, as said below
- particle_level: int32 [1048576], P(('gx', 'gy')), may hold values from 0 to 2, as said below
- les_mean: float32 [53, 64, 1024], P(None, 'gx', 'gy'), may hold values from -6 to 6
- mix_rate: float32 [64, 1024], P('gx', 'gy'), may hold values from 0.1 to 3
- rate_matrix: float32 [3, 53, 53], replicated, may hold values from -0.875 to 0.875
- implicit_map: float32 [3, 53, 53], replicated, may hold values from -0.875 to 0.875
Outputs:
- updated: float32 [53, 1048576], P(None, ('gx', 'gy'))
- cell_means: float32 [53, 64, 1024], P(None, 'gx', 'gy')
The draws below stay inside these ranges and needn't reach their ends.
Inputs may be any that keep to these rules, and one draw needn't show every extreme that they name: `particle_cell`: row 0 is below 64 and row 1 below 1024. With the cells split into blocks of 4 x 128 cells in device order (streamwise block index major), every particle's cell lies within 2 cells, in each grid direction, of the block of the device that holds the particle; the distance 2 is reached on every side that has a neighbouring block. `particle_level`: the share of full-mechanism particles differs from device to device, from none to all.
All inputs are finite; a program needn't handle non-finite values.
Results may differ from the reference program's by a relative error of at most 0.0001.
Values sent between devices are 32-bit elements; how exact they have to be, the bound alone decides.
No kernel may reach another device: no remote copies, remote signals or barrier semaphores. Data moves between devices by JAX's collectives and lax.ppermute only.
A program may use at most 64 MiB of HBM per device.

```python
import math
import jax
import jax.numpy as jnp
from jax import lax

NSP = 53
NS_LOW = 21
NS_MID = 24
CX = 4
CY = 128
R = 2
P_DEV = 8192
P_TOTAL = 1048576
NX = 64
NY = 1024


def draw_particle_cell(key, part):
    grid_rows = NY // CY
    device_id = jnp.arange(P_TOTAL, dtype=jnp.int32) // P_DEV
    column_index = device_id // grid_rows
    row_index = device_id % grid_rows
    key_flagx, key_flagy, key_cellx, key_celly = jax.random.split(key, 4)
    spread_x = jax.random.randint(key_flagx, (P_TOTAL,), 0, 4) == 0
    spread_y = jax.random.randint(key_flagy, (P_TOTAL,), 0, 4) == 0
    lower_x = jnp.where(spread_x, jnp.maximum(column_index * CX - R, 0), column_index * CX)
    upper_x = jnp.where(spread_x, jnp.minimum(column_index * CX + CX + R, NX), column_index * CX + CX)
    lower_y = jnp.where(spread_y, jnp.maximum(row_index * CY - R, 0), row_index * CY)
    upper_y = jnp.where(spread_y, jnp.minimum(row_index * CY + CY + R, NY), row_index * CY + CY)
    cell_x = jax.random.randint(key_cellx, (P_TOTAL,), lower_x, upper_x)
    cell_y = jax.random.randint(key_celly, (P_TOTAL,), lower_y, upper_y)
    return jnp.stack([cell_x, cell_y], 0).astype(jnp.int32)


def draw_particle_level(key, part):
    key_device, key_pick, key_lower = jax.random.split(key, 3)
    device_total = NX // CX * (NY // CY)
    flame_share = jax.random.randint(key_device, (device_total,), 0, 9)
    device_id = jnp.arange(P_TOTAL, dtype=jnp.int32) // P_DEV
    share_each = jnp.take(flame_share, device_id)
    picked = jax.random.randint(key_pick, (P_TOTAL,), 0, 8)
    lower_level = jax.random.randint(key_lower, (P_TOTAL,), 0, 2)
    return jnp.where(picked < share_each, 2, lower_level).astype(jnp.int32)


def level_of(own_key, extent, cuts, smallest, high):
    level, own = 1.0, jax.random.fold_in(own_key, 6)
    for position, shards_of in cuts:
        draws = jnp.exp(jax.random.uniform(jax.random.fold_in(own, position), (shards_of,), jnp.float32, smallest / len(cuts), high / len(cuts)))
        level = level * jnp.repeat(draws, extent[position] // shards_of).reshape([-1 if axis == position else 1 for axis in range(len(extent))])
    return level


def normal_values(rng, extent, scale, bound, cuts=(), kind=jnp.bfloat16):
    result = scale * jax.random.normal(rng, extent, jnp.float32)
    if cuts:
        result = result * level_of(rng, extent, cuts, -0.22, 0.18)
    return jnp.clip(result, -bound, bound).astype(kind)


def setup_inputs(seed: int = 0) -> dict:
    key_of = jax.random.split(jax.random.key(seed), 9)
    composition = normal_values(key_of[0], (NSP, P_TOTAL), 1.0, 6.0, ((1, 128),), jnp.float32)
    particle_mass = jnp.clip(jnp.exp(math.log(3.0) - 2.3025851 * jax.random.uniform(key_of[1], (P_TOTAL,), jnp.float32) ** level_of(key_of[1], (P_TOTAL,), ((0, 128),), -0.2, 0.2)), 0.3, 3.0)
    particle_cell = draw_particle_cell(jax.random.fold_in(key_of[8], 71), 0)
    particle_level = draw_particle_level(jax.random.fold_in(key_of[8], 71), 0)
    les_mean = normal_values(key_of[4], (NSP, NX, NY), 1.0, 6.0, ((1, 16), (2, 8)), jnp.float32)
    mix_rate = jnp.clip(jnp.exp(math.log(3.0) - 3.4011974 * jax.random.uniform(key_of[5], (NX, NY), jnp.float32) ** level_of(key_of[5], (NX, NY), ((0, 16), (1, 8)), -0.2, 0.2)), 0.1, 3.0)
    rate_matrix = normal_values(key_of[6], (3, NSP, NSP), NSP ** -0.5, 0.875, (), jnp.float32)
    implicit_map = normal_values(key_of[7], (3, NSP, NSP), NSP ** -0.5, 0.875, (), jnp.float32)
    return dict(composition=composition, particle_mass=particle_mass, particle_cell=particle_cell, particle_level=particle_level, les_mean=les_mean, mix_rate=mix_rate, rate_matrix=rate_matrix, implicit_map=implicit_map)


prior_weight = 16.0
chem_step = 0.5


def react(mixed_comp, rate_matrix, implicit_map, particle_level):
    updated = mixed_comp
    for tier_index, active in enumerate((NS_LOW, NS_MID, NSP)):
        block_comp = mixed_comp[:active]
        source = jnp.tanh(jnp.dot(rate_matrix[tier_index, :active, :active], block_comp, precision=lax.Precision.HIGHEST, preferred_element_type=jnp.float32))
        change = jnp.dot(implicit_map[tier_index, :active, :active], source, precision=lax.Precision.HIGHEST, preferred_element_type=jnp.float32)
        change = jnp.concatenate([change, jnp.zeros((NSP - active, change.shape[1]), jnp.float32)], 0)
        updated = updated + jnp.where(particle_level[None, :] == tier_index, chem_step * change, 0.0)
    return updated


def reference(composition, particle_mass, particle_cell, particle_level, les_mean, mix_rate, rate_matrix, implicit_map):
    cell_count = NX * NY
    flat_cell = (particle_cell[0] * NY + particle_cell[1]).astype(jnp.int32)
    weighted = composition * particle_mass[None, :]
    weighted_sums = jax.ops.segment_sum(weighted.T, flat_cell, num_segments=cell_count).T.reshape(NSP, NX, NY)
    mass_sums = jax.ops.segment_sum(particle_mass, flat_cell, num_segments=cell_count).reshape(1, NX, NY)
    cell_means = (weighted_sums + prior_weight * les_mean) / (mass_sums + prior_weight)
    particle_means = jnp.take(cell_means.reshape(NSP, cell_count), flat_cell, axis=1)
    particle_rate = jnp.take(mix_rate.reshape(cell_count), flat_cell, axis=0)
    factor = 1.0 - jnp.exp(-particle_rate)
    mixed_comp = composition - factor[None, :] * (composition - particle_means)
    updated = react(mixed_comp, rate_matrix, implicit_map, particle_level)
    return updated, cell_means
```

```python
import functools

import jax
import jax.numpy as jnp
from jax import lax
from jax.experimental import pallas as pl
from jax.experimental.pallas import tpu as pltpu
from jax.sharding import PartitionSpec as P

NS_LOW = 21
NS_MID = 24
NSP = 53
R = 2
CX = 4
CY = 128
ROWS = 56
GROUPS = 4
CHUNK = 1024

prior_weight = 16.0
chem_step = 0.5

f32 = jnp.float32
bf16 = jnp.bfloat16


def split(x):
    high = x.astype(bf16).astype(f32)
    return high, x - high


def stacked(x):
    high, low = split(x)
    return jnp.concatenate([high, low], axis=0).astype(bf16)


def local_cells(cell_ref):
    local_x = cell_ref[0:1, :] - (lax.axis_index("gx") * CX - R)
    local_y = cell_ref[1:2, :] - (lax.axis_index("gy") * CY - R)
    return local_x, local_y


def main_index(local_x, local_y):
    inside = (local_y >= 2 * R) & (local_y < CY)
    return jnp.where(inside, (local_x & 1) * CY + local_y - R, -1)


def edge_index(local_x, local_y):
    low = local_y < 2 * R
    high = local_y >= CY
    place = jnp.where(low, local_y, local_y - CY + 16)
    return jnp.where(low | high, (local_x >> 2) * 32 + (local_x & 3) * 4 + place, -1)


def hot(index, count):
    cells = lax.broadcasted_iota(jnp.int32, (count, index.shape[1]), 0)
    return jnp.where(cells == index, 1.0, 0.0).astype(bf16)


def dot_nt(a, b):
    return lax.dot_general(a, b, (((1,), (1,)), ((), ())), preferred_element_type=f32)


def dot(a, b):
    return jnp.dot(a, b, preferred_element_type=f32)


def sums_kernel(comp_ref, mass_ref, cell_ref, les_ref, rate_ref, main_ref, edge_ref, w_ref):
    step = pl.program_id(0)

    @pl.when(step == 0)
    def _():
        main_ref[...] = jnp.zeros_like(main_ref)
        edge_ref[...] = jnp.zeros_like(edge_ref)
        w_ref[...] = jnp.zeros_like(w_ref)
        lane = lax.broadcasted_iota(jnp.int32, (ROWS, CY), 1)
        inner = (lane >= R) & (lane < CY - R)
        column = lax.broadcasted_iota(jnp.int32, (1, CY), 1)
        for x in range(CX):
            w_ref[0:NSP, 0:CY] = prior_weight * les_ref[:, x, :]
            w_ref[NSP : NSP + 1, 0:CY] = jnp.full((1, CY), prior_weight, f32)
            w_ref[NSP + 1 : NSP + 2, 0:CY] = rate_ref[x : x + 1, :]
            own = w_ref[:, 0:CY]
            group, odd = divmod(x + R, 2)
            main_ref[group * ROWS : (group + 1) * ROWS, odd * CY : (odd + 1) * CY] = jnp.where(
                inner, own, 0.0
            )
            place = hot(edge_index(jnp.full((1, CY), x + R, jnp.int32), column + R), 128)
            both = dot_nt(stacked(own), place)
            edge_ref[...] += both[0:ROWS] + both[ROWS:]
        w_ref[...] = jnp.zeros_like(w_ref)

    mass = mass_ref[...].reshape(1, CHUNK)
    w_ref[0:NSP, :] = comp_ref[...] * mass
    w_ref[NSP : NSP + 1, :] = mass
    w = stacked(w_ref[...])
    local_x, local_y = local_cells(cell_ref)
    place = hot(main_index(local_x, local_y), 2 * CY)
    for group in range(GROUPS):
        mask = jnp.where((local_x >> 1) == group, 1.0, 0.0).astype(bf16)
        both = dot_nt(w * mask, place)
        main_ref[group * ROWS : (group + 1) * ROWS, :] += both[0:ROWS] + both[ROWS:]
    both = dot_nt(w, hot(edge_index(local_x, local_y), 128))
    edge_ref[...] += both[0:ROWS] + both[ROWS:]


def pack_kernel(main_ref, edge_ref, even_in_ref, odd_in_ref, even_ref, odd_ref):
    odd_y = lax.axis_index("gy") % 2 == 1
    odd_x = lax.axis_index("gx") % 2 == 1
    even_in = even_in_ref[...]
    odd_in = odd_in_ref[...]
    upper = jnp.where(odd_y, odd_in, even_in)
    lower = jnp.where(odd_y, even_in, odd_in)
    lane = lax.broadcasted_iota(jnp.int32, (ROWS, 128), 1)
    high = (lane & 16) != 0
    edge = edge_ref[...] + jnp.where(high, pltpu.roll(upper, 16, 1), pltpu.roll(lower, 112, 1))
    half = 2 * ROWS
    left, right = main_ref[0:half, :], main_ref[half:, :]
    even_ref[0:half, :] = jnp.where(odd_x, left, right)
    odd_ref[0:half, :] = jnp.where(odd_x, right, left)
    left_edge, right_edge = edge, pltpu.roll(edge, 96, 1)
    quarter = lane[0:8] >> 5
    for ref, part in (
        (even_ref, jnp.where(odd_x, left_edge, right_edge)),
        (odd_ref, jnp.where(odd_x, right_edge, left_edge)),
    ):
        for side in range(2):
            packed = jnp.zeros((8, 128), f32)
            for k in range(4):
                block = side * 4 + k
                if block < ROWS // 8:
                    rows = part[block * 8 : block * 8 + 8]
                    moved = pltpu.roll(rows, 32 * k, 1) if k else rows
                    packed = jnp.where(quarter == k, moved, packed)
            ref[half : half + 8, side * 128 : (side + 1) * 128] = packed


def table(total):
    rows = lax.broadcasted_iota(jnp.int32, total.shape, 0)
    mass = total[NSP : NSP + 1]
    mass = jnp.where(mass > 0.0, mass, 1.0)
    means = total / mass
    keep = jnp.exp(-total[NSP + 1 : NSP + 2])
    return means, jnp.where(rows < NSP, (1.0 - keep) * means, jnp.where(rows == NSP, keep, 0.0))


def unpacked(packed):
    lane = lax.broadcasted_iota(jnp.int32, (8, 128), 1)
    blocks = []
    for block in range(ROWS // 8):
        side, k = divmod(block, 4)
        rows = packed[:, side * 128 : (side + 1) * 128]
        rows = pltpu.roll(rows, 128 - 32 * k, 1) if k else rows
        blocks.append(jnp.where(lane < 32, rows, 0.0))
    return jnp.concatenate(blocks, axis=0)


def operator_rows(matrix_ref, full_ref, out_ref, scale):
    full_ref[...] = jnp.zeros_like(full_ref)
    start = 0
    for level, active in enumerate((NS_LOW, NS_MID, NSP)):
        rows = -(-active // 8) * 8
        count = min(rows, NSP)
        row = lax.broadcasted_iota(jnp.int32, (count, NSP), 0)
        col = lax.broadcasted_iota(jnp.int32, (count, NSP), 1)
        block = matrix_ref[level, 0:count, :] * scale
        high, low = split(jnp.where((row < active) & (col < active), block, 0.0))
        full_ref[start : start + count, 0:NSP] = high
        full_ref[start : start + count, 64 : 64 + NSP] = high
        full_ref[start : start + count, 128 : 128 + NSP] = low
        start += rows
    out_ref[...] = full_ref[...].astype(bf16)


def three(x):
    high, low = split(x)
    return jnp.concatenate([high, low, high], axis=0).astype(bf16)


def react_kernel(
    even_ref,
    odd_ref,
    even_in_ref,
    odd_in_ref,
    rate_ref,
    map_ref,
    comp_ref,
    cell_ref,
    level_ref,
    updated_ref,
    means_ref,
    high_ref,
    low_ref,
    edge_ref,
    full_ref,
    ops_ref,
    maps_ref,
    mixed_ref,
):
    step = pl.program_id(0)
    half = 2 * ROWS

    @pl.when(step == 0)
    def _():
        odd_x = lax.axis_index("gx") % 2 == 1
        even = even_ref[...] + even_in_ref[...]
        odd = odd_ref[...] + odd_in_ref[...]
        left = jnp.where(odd_x, even, odd)
        right = jnp.where(odd_x, odd, even)
        edge = unpacked(left[half:, :]) + pltpu.roll(unpacked(right[half:, :]), 32, 1)
        edge_means, edge_table = table(edge)
        high, low = split(edge_table)
        lane = lax.broadcasted_iota(jnp.int32, (ROWS, 128), 1)
        edge_ref[...] = jnp.where(lane < 64, high, pltpu.roll(low, 64, 1)).astype(bf16)
        high, low = split(edge_means)
        edge_means = jnp.where(lane < 64, high, pltpu.roll(low, 64, 1)).astype(bf16)
        row = lax.broadcasted_iota(jnp.int32, (128, CY), 0) & 63
        col = lax.broadcasted_iota(jnp.int32, (1, CY), 1)
        inner = (lane >= R) & (lane < CY - R)
        for group in range(GROUPS):
            source = left if group < 2 else right
            start = (group % 2) * ROWS
            means, cells = table(source[start : start + ROWS])
            high, low = split(cells)
            high_ref[group * ROWS : (group + 1) * ROWS, :] = high
            low_ref[group * ROWS : (group + 1) * ROWS, :] = low
            if group in (1, 2):
                for odd_column in range(2):
                    x = group * 2 + odd_column - R
                    index = edge_index(jnp.full((1, CY), x + R, jnp.int32), col + R)
                    placed = dot(edge_means, jnp.where(row == index, 1.0, 0.0).astype(bf16))
                    own = jnp.where(inner, means[:, odd_column * CY : (odd_column + 1) * CY], placed)
                    means_ref[:, x, :] = own[0:NSP]
        operator_rows(rate_ref, full_ref, ops_ref, 1.0)
        operator_rows(map_ref, full_ref, maps_ref, chem_step)
        mixed_ref[...] = jnp.zeros_like(mixed_ref)

    local_x, local_y = local_cells(cell_ref)
    place = hot(main_index(local_x, local_y), 2 * CY)
    gathered = dot(high_ref[...].astype(bf16), place) + dot(low_ref[...].astype(bf16), place)
    edge_cells = edge_index(local_x, local_y)
    row = lax.broadcasted_iota(jnp.int32, (128, CHUNK), 0) & 63
    value = dot(edge_ref[...], jnp.where(row == edge_cells, 1.0, 0.0).astype(bf16))
    group_of = local_x >> 1
    chosen = gathered[0:ROWS]
    for group in range(1, GROUPS):
        chosen = jnp.where(group_of == group, gathered[group * ROWS : (group + 1) * ROWS], chosen)
    value = value + chosen
    mixed_ref[0:NSP, :] = comp_ref[...] * value[NSP : NSP + 1] + value[0:NSP]
    level = level_ref[...].reshape(1, CHUNK)
    first, second = level == 0, level == 1
    z = dot(ops_ref[...], three(mixed_ref[...]))
    z = jnp.concatenate(
        [jnp.where(first, z[0:24], jnp.where(second, z[24:48], z[48:72])), z[72:104]], axis=0
    )
    source = jnp.concatenate([jnp.tanh(z), jnp.zeros((8, CHUNK), f32)], axis=0)
    z = dot(maps_ref[...], three(source))
    change = jnp.concatenate(
        [
            jnp.where(first, z[0:24], jnp.where(second, z[24:48], z[48:72])),
            jnp.where(level == 2, z[72:104], 0.0),
        ],
        axis=0,
    )
    updated_ref[...] = mixed_ref[0:NSP, :] + change[0:NSP]


def swap(x, axis, odd):
    count = lax.axis_size(axis)
    pairs = [(i, i + 1) for i in range(odd, count - 1, 2)]
    return lax.ppermute(x, axis, pairs + [(b, a) for a, b in pairs])


def whole(shape):
    return pl.BlockSpec(shape, lambda i: (0,) * len(shape))


def per_device(
    composition,
    particle_mass,
    particle_cell,
    particle_level,
    les_mean,
    mix_rate,
    rate_matrix,
    implicit_map,
):
    particles = composition.shape[1]
    grid = (particles // CHUNK,)
    columns = lambda rows: pl.BlockSpec((rows, CHUNK), lambda i: (0, i))
    line = pl.BlockSpec((CHUNK,), lambda i: (i,))
    sds = jax.ShapeDtypeStruct
    main, edge = pl.pallas_call(
        sums_kernel,
        grid=grid,
        out_shape=(sds((GROUPS * ROWS, 2 * CY), f32), sds((ROWS, 128), f32)),
        in_specs=[columns(NSP), line, columns(2), whole((NSP, CX, CY)), whole((CX, CY))],
        out_specs=(whole((GROUPS * ROWS, 2 * CY)), whole((ROWS, 128))),
        scratch_shapes=[pltpu.VMEM((ROWS, CHUNK), f32)],
        compiler_params=pltpu.CompilerParams(vmem_limit_bytes=32 << 20),
        name="cell_sums",
    )(composition, particle_mass, particle_cell, les_mean, mix_rate)
    edge_even = swap(edge, "gy", 0)
    edge_odd = swap(edge, "gy", 1)
    payload = sds((2 * ROWS + 8, 2 * CY), f32)
    even, odd = pl.pallas_call(
        pack_kernel,
        out_shape=(payload, payload),
        compiler_params=pltpu.CompilerParams(vmem_limit_bytes=32 << 20),
        name="pack",
    )(main, edge, edge_even, edge_odd)
    even_in = swap(even, "gx", 0)
    odd_in = swap(odd, "gx", 1)
    updated, means = pl.pallas_call(
        react_kernel,
        grid=grid,
        out_shape=(sds(composition.shape, f32), sds(les_mean.shape, f32)),
        in_specs=[whole(payload.shape)] * 4
        + [whole(rate_matrix.shape)] * 2
        + [columns(NSP), columns(2), line],
        out_specs=(columns(NSP), whole(les_mean.shape)),
        scratch_shapes=[
            pltpu.VMEM((GROUPS * ROWS, 2 * CY), f32),
            pltpu.VMEM((GROUPS * ROWS, 2 * CY), f32),
            pltpu.VMEM((ROWS, 128), bf16),
            pltpu.VMEM((104, 192), f32),
            pltpu.VMEM((104, 192), bf16),
            pltpu.VMEM((104, 192), bf16),
            pltpu.VMEM((64, CHUNK), f32),
        ],
        compiler_params=pltpu.CompilerParams(vmem_limit_bytes=32 << 20),
        name="gather_react",
    )(even, odd, even_in, odd_in, rate_matrix, implicit_map, composition, particle_cell, particle_level)
    return updated, means


def solution(mesh):
    placed = (
        P(None, ("gx", "gy")),
        P(("gx", "gy")),
        P(None, ("gx", "gy")),
        P(("gx", "gy")),
        P(None, "gx", "gy"),
        P("gx", "gy"),
        P(),
        P(),
    )
    return jax.shard_map(
        per_device,
        mesh=mesh,
        in_specs=placed,
        out_specs=(P(None, ("gx", "gy")), P(None, "gx", "gy")),
        check_vma=False,
    )
```

```python
import jax
import jax.numpy as jnp
from jax import lax
from jax.experimental import pallas as pl
from jax.experimental.pallas import tpu as pltpu
from jax.sharding import PartitionSpec as P

NS_LOW = 21
NS_MID = 24
NSP = 53
R = 2
CX = 4
CY = 128
ROWS = 56
GROUPS = 4
BANDS = GROUPS + 1
PART = 2048
CHUNK = 4096
VMEM = pltpu.CompilerParams(vmem_limit_bytes=40 << 20)

prior_weight = 16.0
chem_step = 0.5

f32 = jnp.float32
bf16 = jnp.bfloat16


def split(x):
    high = x.astype(bf16).astype(f32)
    return high, x - high


def stacked(x):
    high, low = split(x)
    return jnp.concatenate([high, low], axis=0).astype(bf16)


def local_cells(cells):
    local_x = cells[0:1, :] - (lax.axis_index("gx") * CX - R)
    local_y = cells[1:2, :] - (lax.axis_index("gy") * CY - R)
    return local_x, local_y


def edge_index(local_x, local_y):
    place = jnp.where(local_y < 2 * R, local_y, local_y - CY + 16)
    return (local_x >> 2) * 32 + (local_x & 3) * 4 + place


def band_and_index(local_x, local_y):
    inside = (local_y >= 2 * R) & (local_y < CY)
    band = jnp.where(inside, local_x >> 1, GROUPS)
    index = jnp.where(inside, (local_x & 1) * CY + local_y - R, edge_index(local_x, local_y))
    return band, index


def hot(index, count):
    cells = lax.broadcasted_iota(jnp.int32, (count, index.shape[1]), 0)
    return jnp.where(cells == index, 1.0, 0.0).astype(bf16)


def dot_nt(a, b):
    return lax.dot_general(a, b, (((1,), (1,)), ((), ())), preferred_element_type=f32)


def dot(a, b):
    return jnp.dot(a, b, preferred_element_type=f32)


def sums_kernel(
    comp_hbm, mass_hbm, cell_hbm, les_hbm, rate_hbm, main_ref, edge_ref, comp_ref,
    mass_ref, cell_ref, les_ref, rate_ref, w_ref, sems,
):
    particles = comp_ref.shape[1]
    parts = particles // PART
    pairs = [(les_hbm, les_ref), (rate_hbm, rate_ref), (cell_hbm, cell_ref), (mass_hbm, mass_ref)]
    small = len(pairs)
    for part in range(parts):
        at = pl.ds(part * PART, PART)
        pairs.append((comp_hbm.at[:, at], comp_ref.at[:, at]))
    copies = [pltpu.make_async_copy(src, dst, sems.at[i]) for i, (src, dst) in enumerate(pairs)]
    for copy in copies:
        copy.start()
    w_ref[...] = jnp.zeros_like(w_ref)
    main_ref[...] = jnp.zeros_like(main_ref)
    lane = lax.broadcasted_iota(jnp.int32, (ROWS, CY), 1)
    inner = (lane >= R) & (lane < CY - R)
    cells = CX * CY
    cell = lax.broadcasted_iota(jnp.int32, (1, cells), 1)
    band, index = band_and_index(cell // CY + R, cell % CY + R)
    place = hot(jnp.where(band == GROUPS, index, -1), 128)
    copies[0].wait()
    copies[1].wait()
    for x in range(CX):
        at = slice(x * CY, (x + 1) * CY)
        w_ref[0:NSP, at] = prior_weight * les_ref[:, x, :]
        w_ref[NSP : NSP + 1, at] = jnp.full((1, CY), prior_weight, f32)
        w_ref[NSP + 1 : NSP + 2, at] = rate_ref[x : x + 1, :]
        band, odd = divmod(x + R, 2)
        where = (slice(band * ROWS, (band + 1) * ROWS), slice(odd * CY, (odd + 1) * CY))
        main_ref[where] = jnp.where(inner, w_ref[:, at], 0.0)
    both = dot_nt(stacked(w_ref[:, 0:cells]), place)
    edge_ref[...] = both[0:ROWS] + both[ROWS:]
    w_ref[NSP : NSP + 2, :] = jnp.zeros((2, PART), f32)
    copies[2].wait()
    copies[3].wait()
    for part in range(parts):
        copies[small + part].wait()
        at = pl.ds(part * PART, PART)
        mass = mass_ref[at].reshape(1, PART)
        w_ref[0:NSP, :] = comp_ref[:, at] * mass
        w_ref[NSP : NSP + 1, :] = mass
        w = stacked(w_ref[...])
        band, index = band_and_index(*local_cells(cell_ref[:, at]))
        banded = [w * jnp.where(band == k, 1.0, 0.0).astype(bf16) for k in range(BANDS)]
        both = dot_nt(jnp.concatenate(banded, axis=0), hot(index, 2 * CY))
        for k in range(BANDS):
            start = 2 * ROWS * k
            sums = both[start : start + ROWS] + both[start + ROWS : start + 2 * ROWS]
            if k < GROUPS:
                main_ref[k * ROWS : (k + 1) * ROWS, :] += sums
            else:
                edge_ref[...] += sums[:, 0:128]


def pack_kernel(main_ref, edge_ref, even_in_ref, odd_in_ref, even_ref, odd_ref):
    odd_y = lax.axis_index("gy") % 2 == 1
    odd_x = lax.axis_index("gx") % 2 == 1
    even_in = even_in_ref[...]
    odd_in = odd_in_ref[...]
    row = lax.axis_index("gy")
    upper = jnp.where(row < lax.axis_size("gy") - 1, jnp.where(odd_y, odd_in, even_in), 0.0)
    lower = jnp.where(row > 0, jnp.where(odd_y, even_in, odd_in), 0.0)
    lane = lax.broadcasted_iota(jnp.int32, (ROWS, 128), 1)
    high = (lane & 16) != 0
    edge = edge_ref[...] + jnp.where(high, pltpu.roll(upper, 16, 1), pltpu.roll(lower, 112, 1))
    half = 2 * ROWS
    left, right = main_ref[0:half, :], main_ref[half:, :]
    even_ref[0:half, :] = jnp.where(odd_x, left, right)
    odd_ref[0:half, :] = jnp.where(odd_x, right, left)
    left_edge, right_edge = edge, pltpu.roll(edge, 96, 1)
    quarter = lane[0:8] >> 5
    for ref, part in (
        (even_ref, jnp.where(odd_x, left_edge, right_edge)),
        (odd_ref, jnp.where(odd_x, right_edge, left_edge)),
    ):
        for side in range(2):
            packed = jnp.zeros((8, 128), f32)
            for k in range(4):
                block = side * 4 + k
                if block < ROWS // 8:
                    rows = part[block * 8 : block * 8 + 8]
                    moved = pltpu.roll(rows, 32 * k, 1) if k else rows
                    packed = jnp.where(quarter == k, moved, packed)
            ref[half : half + 8, side * 128 : (side + 1) * 128] = packed


def table(total):
    rows = lax.broadcasted_iota(jnp.int32, total.shape, 0)
    mass = total[NSP : NSP + 1]
    mass = jnp.where(mass > 0.0, mass, 1.0)
    means = total / mass
    keep = jnp.exp(-total[NSP + 1 : NSP + 2])
    return means, jnp.where(rows < NSP, (1.0 - keep) * means, jnp.where(rows == NSP, keep, 0.0))


def unpacked(packed):
    lane = lax.broadcasted_iota(jnp.int32, (8, 128), 1)
    blocks = []
    for block in range(ROWS // 8):
        side, k = divmod(block, 4)
        rows = packed[:, side * 128 : (side + 1) * 128]
        rows = pltpu.roll(rows, 128 - 32 * k, 1) if k else rows
        blocks.append(jnp.where(lane < 32, rows, 0.0))
    return jnp.concatenate(blocks, axis=0)


def operator_rows(matrix_ref, full_ref, out_ref, scale):
    full_ref[...] = jnp.zeros_like(full_ref)
    start = 0
    for level, active in enumerate((NS_LOW, NS_MID, NSP)):
        rows = -(-active // 8) * 8
        count = min(rows, NSP)
        row = lax.broadcasted_iota(jnp.int32, (count, NSP), 0)
        col = lax.broadcasted_iota(jnp.int32, (count, NSP), 1)
        block = matrix_ref[level, 0:count, :] * scale
        high, low = split(jnp.where((row < active) & (col < active), block, 0.0))
        full_ref[start : start + count, 0:NSP] = high
        full_ref[start : start + count, 64 : 64 + NSP] = high
        full_ref[start : start + count, 128 : 128 + NSP] = low
        start += rows
    out_ref[...] = full_ref[...].astype(bf16)


def three(x):
    high, low = split(x)
    return jnp.concatenate([high, low, high], axis=0).astype(bf16)


def prepare_kernel(cell_ref, level_ref, rate_ref, map_ref, hot_ref, which_ref, ops_ref, maps_ref, full_ref):
    operator_rows(rate_ref, full_ref, ops_ref, 1.0)
    operator_rows(map_ref, full_ref, maps_ref, chem_step)
    particles = cell_ref.shape[1]
    which_ref[1:2, :] = level_ref[...].reshape(1, particles)

    def body(i, carry):
        at = pl.ds(pl.multiple_of(i * CHUNK, CHUNK), CHUNK)
        band, index = band_and_index(*local_cells(cell_ref[:, at]))
        which_ref[0:1, at] = band
        hot_ref[:, at] = hot(index, 2 * CY)
        return carry

    lax.fori_loop(0, particles // CHUNK, body, 0)


def react_kernel(
    even_ref, odd_ref, even_in_ref, odd_in_ref, ops_ref, maps_ref, hot_ref, which_ref, comp_ref,
    updated_hbm, means_hbm,
    means_ref, full_ref, cells_ref, mixed_ref, out_ref, sems,
):
    half = 2 * ROWS
    odd_x = lax.axis_index("gx") % 2 == 1
    even = even_ref[...] + even_in_ref[...]
    column = lax.axis_index("gx")
    at_end = (column == 0) | (column == lax.axis_size("gx") - 1)
    odd = odd_ref[...] + jnp.where(at_end, 0.0, odd_in_ref[...])
    left = jnp.where(odd_x, even, odd)
    right = jnp.where(odd_x, odd, even)
    edge = unpacked(left[half:, :]) + pltpu.roll(unpacked(right[half:, :]), 32, 1)
    lane = lax.broadcasted_iota(jnp.int32, (ROWS, 128), 1)
    edge_means, edge_table = table(edge)
    start = GROUPS * half
    full_ref[start:, 128:] = jnp.zeros((half, 128), f32)
    high, low = split(jnp.where(lane < 64, edge_table, 0.0))
    full_ref[start : start + ROWS, 0:128] = high
    full_ref[start + ROWS :, 0:128] = low
    high, low = split(edge_means)
    edge_means = jnp.where(lane < 64, high, pltpu.roll(low, 64, 1)).astype(bf16)
    row = lax.broadcasted_iota(jnp.int32, (128, CY), 0) & 63
    col = lax.broadcasted_iota(jnp.int32, (1, CY), 1)
    inner = (lane >= R) & (lane < CY - R)
    for group in range(GROUPS):
        source = left if group < 2 else right
        start = (group % 2) * ROWS
        means, cells = table(source[start : start + ROWS])
        high, low = split(cells)
        full_ref[group * half : group * half + ROWS, :] = high
        full_ref[group * half + ROWS : (group + 1) * half, :] = low
        if group in (1, 2):
            for odd_column in range(2):
                x = group * 2 + odd_column - R
                index = edge_index(jnp.full((1, CY), x + R, jnp.int32), col + R)
                placed = dot(edge_means, jnp.where(row == index, 1.0, 0.0).astype(bf16))
                own = jnp.where(inner, means[:, odd_column * CY : (odd_column + 1) * CY], placed)
                means_ref[:, x, :] = own[0:NSP]
    means_copy = pltpu.make_async_copy(means_ref, means_hbm, sems.at[0])
    means_copy.start()
    cells_ref[...] = full_ref[...].astype(bf16)
    mixed_ref[...] = jnp.zeros_like(mixed_ref)
    chunks = comp_ref.shape[1] // CHUNK

    def copy_of(chunk):
        at = pl.ds(chunk * CHUNK, CHUNK)
        return pltpu.make_async_copy(out_ref.at[:, at], updated_hbm.at[:, at], sems.at[1 + chunk])

    for chunk in range(chunks):
        at = pl.ds(chunk * CHUNK, CHUNK)
        gathered = dot(cells_ref[...], hot_ref[:, at])
        band = which_ref[0:1, at]
        chosen = gathered[0:half]
        for k in range(1, BANDS):
            chosen = jnp.where(band == k, gathered[k * half : (k + 1) * half], chosen)
        value = chosen[0:ROWS] + chosen[ROWS:]
        mixed_ref[0:NSP, :] = comp_ref[:, at] * value[NSP : NSP + 1] + value[0:NSP]
        level = which_ref[1:2, at]
        first, second = level == 0, level == 1
        z = dot(ops_ref[...], three(mixed_ref[...]))
        z = jnp.concatenate(
            [jnp.where(first, z[0:24], jnp.where(second, z[24:48], z[48:72])), z[72:104]], axis=0
        )
        source = jnp.concatenate([jnp.tanh(z), jnp.zeros((8, CHUNK), f32)], axis=0)
        z = dot(maps_ref[...], three(source))
        change = jnp.concatenate(
            [
                jnp.where(first, z[0:24], jnp.where(second, z[24:48], z[48:72])),
                jnp.where(level == 2, z[72:104], 0.0),
            ],
            axis=0,
        )
        out_ref[:, at] = mixed_ref[0:NSP, :] + change[0:NSP]
        copy_of(chunk).start()
    means_copy.wait()
    for chunk in range(chunks):
        copy_of(chunk).wait()


def swap(x, axis, odd):
    columns, rows = lax.axis_size("gx"), lax.axis_size("gy")

    def partner(i, j):
        at, count = (i, columns) if axis == "gx" else (j, rows)
        other = at + 1 if at % 2 == odd else at - 1
        if axis == "gx":
            return (other, j) if 0 <= other < count else (i, j ^ 1)
        return (i, other) if 0 <= other < count else (i ^ 1, j)

    pairs = []
    for i in range(columns):
        for j in range(rows):
            k, m = partner(i, j)
            pairs.append((i * rows + j, k * rows + m))
    return lax.ppermute(x, ("gx", "gy"), pairs)


def per_device(
    composition,
    particle_mass,
    particle_cell,
    particle_level,
    les_mean,
    mix_rate,
    rate_matrix,
    implicit_map,
):
    particles = composition.shape[1]
    parts = particles // PART
    sds = jax.ShapeDtypeStruct
    stay = lambda x: pltpu.with_memory_space_constraint(x, pltpu.HBM)
    hbm = pl.BlockSpec(memory_space=pltpu.HBM)
    vmem = pl.BlockSpec(memory_space=pltpu.VMEM)
    main, edge, local = pl.pallas_call(
        sums_kernel,
        out_shape=(
            sds((GROUPS * ROWS, 2 * CY), f32),
            sds((ROWS, 128), f32),
            sds(composition.shape, f32),
        ),
        in_specs=[hbm] * 5,
        out_specs=(vmem,) * 3,
        scratch_shapes=[
            pltpu.VMEM(particle_mass.shape, f32),
            pltpu.VMEM(particle_cell.shape, jnp.int32),
            pltpu.VMEM(les_mean.shape, f32),
            pltpu.VMEM(mix_rate.shape, f32),
            pltpu.VMEM((ROWS, PART), f32),
            pltpu.SemaphoreType.DMA((parts + 4,)),
        ],
        compiler_params=VMEM,
        name="cell_sums",
    )(*map(stay, (composition, particle_mass, particle_cell, les_mean, mix_rate)))
    edge_even = swap(edge, "gy", 0)
    edge_odd = swap(edge, "gy", 1)
    payload = sds((2 * ROWS + 8, 2 * CY), f32)
    even, odd = pl.pallas_call(
        pack_kernel,
        out_shape=(payload, payload),
        compiler_params=VMEM,
        name="pack",
    )(main, edge, edge_even, edge_odd)
    even_in = swap(even, "gx", 0)
    odd_in = swap(odd, "gx", 1)
    operator = sds((104, 192), bf16)
    places, which, ops, maps = pl.pallas_call(
        prepare_kernel,
        out_shape=(sds((2 * CY, particles), bf16), sds((2, particles), jnp.int32), operator, operator),
        in_specs=[vmem] * 4,
        out_specs=(vmem,) * 4,
        scratch_shapes=[pltpu.VMEM((104, 192), f32)],
        compiler_params=VMEM,
        cost_estimate=pl.CostEstimate(flops=1 << 22, bytes_accessed=8 << 20, transcendentals=0),
        name="prepare",
    )(particle_cell, particle_level, rate_matrix, implicit_map)
    return pl.pallas_call(
        react_kernel,
        out_shape=(sds(composition.shape, f32), sds(les_mean.shape, f32)),
        in_specs=[vmem] * 9,
        out_specs=(hbm, hbm),
        scratch_shapes=[
            pltpu.VMEM(les_mean.shape, f32),
            pltpu.VMEM((BANDS * 2 * ROWS, 2 * CY), f32),
            pltpu.VMEM((BANDS * 2 * ROWS, 2 * CY), bf16),
            pltpu.VMEM((64, CHUNK), f32),
            pltpu.VMEM(composition.shape, f32),
            pltpu.SemaphoreType.DMA((particles // CHUNK + 1,)),
        ],
        compiler_params=VMEM,
        name="gather_react",
    )(even, odd, even_in, odd_in, ops, maps, places, which, local)


def solution(mesh):
    placed = (
        P(None, ("gx", "gy")),
        P(("gx", "gy")),
        P(None, ("gx", "gy")),
        P(("gx", "gy")),
        P(None, "gx", "gy"),
        P("gx", "gy"),
        P(),
        P(),
    )
    return jax.shard_map(
        per_device,
        mesh=mesh,
        in_specs=placed,
        out_specs=(P(None, ("gx", "gy")), P(None, "gx", "gy")),
        check_vma=False,
    )
```

```python
import jax
import jax.numpy as jnp
from jax import lax
from jax.experimental import pallas as pl
from jax.experimental.pallas import tpu as pltpu
from jax.sharding import PartitionSpec as P

NS_LOW = 21
NS_MID = 24
NSP = 53
R = 2
CX = 4
CY = 128
ROWS = 56
GROUPS = 4
BANDS = GROUPS + 1
ROWBLOCK = 8
CHUNK = 4096
VMEM = pltpu.CompilerParams(vmem_limit_bytes=40 << 20)

prior_weight = 16.0
chem_step = 0.5

f32 = jnp.float32
bf16 = jnp.bfloat16


def split(x):
    high = x.astype(bf16).astype(f32)
    return high, x - high


def stacked(x):
    high, low = split(x)
    return jnp.concatenate([high, low], axis=0).astype(bf16)


def local_cells(cells):
    local_x = cells[0:1, :] - (lax.axis_index("gx") * CX - R)
    local_y = cells[1:2, :] - (lax.axis_index("gy") * CY - R)
    return local_x, local_y


def edge_index(local_x, local_y):
    place = jnp.where(local_y < 2 * R, local_y, local_y - CY + 16)
    return (local_x >> 2) * 32 + (local_x & 3) * 4 + place


def band_and_index(local_x, local_y):
    inside = (local_y >= 2 * R) & (local_y < CY)
    band = jnp.where(inside, local_x >> 1, GROUPS)
    index = jnp.where(inside, (local_x & 1) * CY + local_y - R, edge_index(local_x, local_y))
    return band, index


def hot(index, count):
    cells = lax.broadcasted_iota(jnp.int32, (count, index.shape[1]), 0)
    return jnp.where(cells == index, 1.0, 0.0).astype(bf16)


def dot_nt(a, b):
    return lax.dot_general(a, b, (((1,), (1,)), ((), ())), preferred_element_type=f32)


def dot(a, b):
    return jnp.dot(a, b, preferred_element_type=f32)


def sums_kernel(
    comp_hbm, mass_hbm, cell_hbm, les_hbm, rate_hbm, main_ref, edge_ref, comp_ref,
    mass_ref, cell_ref, les_ref, rate_ref, w_ref, hot_ref, sems,
):
    particles = comp_ref.shape[1]
    pairs = [(les_hbm, les_ref), (rate_hbm, rate_ref), (cell_hbm, cell_ref), (mass_hbm, mass_ref)]
    for start in range(0, NSP, ROWBLOCK):
        at = pl.ds(start, min(ROWBLOCK, NSP - start))
        pairs.append((comp_hbm.at[at], comp_ref.at[at]))
    copies = [pltpu.make_async_copy(src, dst, sems.at[i]) for i, (src, dst) in enumerate(pairs)]
    for copy in copies:
        copy.start()
    w_ref[NSP:, :] = jnp.zeros((ROWS - NSP, particles), f32)
    main_ref[...] = jnp.zeros_like(main_ref)
    lane = lax.broadcasted_iota(jnp.int32, (ROWS, CY), 1)
    inner = (lane >= R) & (lane < CY - R)
    cells = CX * CY
    cell = lax.broadcasted_iota(jnp.int32, (1, cells), 1)
    band, index = band_and_index(cell // CY + R, cell % CY + R)
    place = hot(jnp.where(band == GROUPS, index, -1), 128)
    copies[0].wait()
    copies[1].wait()
    for x in range(CX):
        at = slice(x * CY, (x + 1) * CY)
        w_ref[0:NSP, at] = prior_weight * les_ref[:, x, :]
        w_ref[NSP : NSP + 1, at] = jnp.full((1, CY), prior_weight, f32)
        w_ref[NSP + 1 : NSP + 2, at] = rate_ref[x : x + 1, :]
        band, odd = divmod(x + R, 2)
        where = (slice(band * ROWS, (band + 1) * ROWS), slice(odd * CY, (odd + 1) * CY))
        main_ref[where] = jnp.where(inner, w_ref[:, at], 0.0)
    both = dot_nt(stacked(w_ref[:, 0:cells]), place)
    edge = both[0:ROWS] + both[ROWS:]
    w_ref[NSP : NSP + 2, :] = jnp.zeros((2, particles), f32)
    for copy in copies[2:]:
        copy.wait()
    mass = mass_ref[...].reshape(1, particles)
    band, index = band_and_index(*local_cells(cell_ref[...]))
    w_ref[0:NSP, :] = comp_ref[...] * mass
    w_ref[NSP : NSP + 1, :] = mass
    w = stacked(w_ref[...])
    banded = [w * jnp.where(band == k, 1.0, 0.0).astype(bf16) for k in range(BANDS)]
    both = dot_nt(jnp.concatenate(banded, axis=0), hot(index, 2 * CY))
    for k in range(BANDS):
        start = 2 * ROWS * k
        sums = both[start : start + ROWS] + both[start + ROWS : start + 2 * ROWS]
        if k < GROUPS:
            main_ref[k * ROWS : (k + 1) * ROWS, :] += sums
        else:
            edge += sums[:, 0:128]
    rest = pltpu.roll(jnp.concatenate([edge[32:], jnp.zeros((8, 128), f32)], axis=0), 64, 1)
    edge_ref[...] = jnp.where(lane[0:32] < 64, edge[0:32], rest)


def pack_kernel(main_ref, edge_ref, even_in_ref, odd_in_ref, odd_ref, even_ref):
    odd_y = lax.axis_index("gy") % 2 == 1
    odd_x = lax.axis_index("gx") % 2 == 1
    even_in = even_in_ref[...]
    odd_in = odd_in_ref[...]
    row = lax.axis_index("gy")
    upper = jnp.where(row < lax.axis_size("gy") - 1, jnp.where(odd_y, odd_in, even_in), 0.0)
    lower = jnp.where(row > 0, jnp.where(odd_y, even_in, odd_in), 0.0)
    lane = lax.broadcasted_iota(jnp.int32, (32, 128), 1)
    high = (lane & 16) != 0
    both = edge_ref[...] + jnp.where(high, pltpu.roll(upper, 16, 1), pltpu.roll(lower, 112, 1))
    edge = jnp.concatenate([both, pltpu.roll(both, 64, 1)[0 : ROWS - 32]], axis=0)
    half = 2 * ROWS
    left, right = main_ref[0:half, :], main_ref[half:, :]
    even_ref[0:half, :] = jnp.where(odd_x, left, right)
    odd_ref[0:half, :] = jnp.where(odd_x, right, left)
    left_edge, right_edge = edge, pltpu.roll(edge, 96, 1)
    quarter = lane[0:8] >> 5
    for ref, part in (
        (even_ref, jnp.where(odd_x, left_edge, right_edge)),
        (odd_ref, jnp.where(odd_x, right_edge, left_edge)),
    ):
        for side in range(2):
            packed = jnp.zeros((8, 128), f32)
            for k in range(4):
                block = side * 4 + k
                if block < ROWS // 8:
                    rows = part[block * 8 : block * 8 + 8]
                    moved = pltpu.roll(rows, 32 * k, 1) if k else rows
                    packed = jnp.where(quarter == k, moved, packed)
            ref[half : half + 8, side * 128 : (side + 1) * 128] = packed


def table(total):
    rows = lax.broadcasted_iota(jnp.int32, total.shape, 0)
    mass = total[NSP : NSP + 1]
    mass = jnp.where(mass > 0.0, mass, 1.0)
    means = total / mass
    keep = jnp.exp(-total[NSP + 1 : NSP + 2])
    return means, jnp.where(rows < NSP, (1.0 - keep) * means, jnp.where(rows == NSP, keep, 0.0))


def unpacked(packed):
    lane = lax.broadcasted_iota(jnp.int32, (8, 128), 1)
    blocks = []
    for block in range(ROWS // 8):
        side, k = divmod(block, 4)
        rows = packed[:, side * 128 : (side + 1) * 128]
        rows = pltpu.roll(rows, 128 - 32 * k, 1) if k else rows
        blocks.append(jnp.where(lane < 32, rows, 0.0))
    return jnp.concatenate(blocks, axis=0)


def operator_rows(matrix_ref, full_ref, out_ref, scale):
    full_ref[...] = jnp.zeros_like(full_ref)
    start = 0
    for level, active in enumerate((NS_LOW, NS_MID, NSP)):
        rows = -(-active // 8) * 8
        count = min(rows, NSP)
        row = lax.broadcasted_iota(jnp.int32, (count, NSP), 0)
        col = lax.broadcasted_iota(jnp.int32, (count, NSP), 1)
        block = matrix_ref[level, 0:count, :] * scale
        high, low = split(jnp.where((row < active) & (col < active), block, 0.0))
        full_ref[start : start + count, 0:NSP] = high
        full_ref[start : start + count, 64 : 64 + NSP] = high
        full_ref[start : start + count, 128 : 128 + NSP] = low
        start += rows
    out_ref[...] = full_ref[...].astype(bf16)


def three(x):
    high, low = split(x)
    return jnp.concatenate([high, low, high], axis=0).astype(bf16)


def prepare_kernel(cell_ref, level_ref, rate_ref, map_ref, hot_ref, which_ref, ops_ref, maps_ref, full_ref):
    operator_rows(rate_ref, full_ref, ops_ref, 1.0)
    operator_rows(map_ref, full_ref, maps_ref, chem_step)
    particles = cell_ref.shape[1]
    which_ref[1:2, :] = level_ref[...].reshape(1, particles)

    def body(i, carry):
        at = pl.ds(pl.multiple_of(i * CHUNK, CHUNK), CHUNK)
        band, index = band_and_index(*local_cells(cell_ref[:, at]))
        which_ref[0:1, at] = band
        hot_ref[:, at] = hot(index, 2 * CY)
        return carry

    lax.fori_loop(0, particles // CHUNK, body, 0)


def react_kernel(
    odd_ref, even_ref, odd_in_ref, even_in_ref, ops_ref, maps_ref, hot_ref, which_ref, comp_ref,
    updated_hbm, means_hbm,
    means_ref, full_ref, cells_ref, mixed_ref, out_ref, sems,
):
    half = 2 * ROWS
    odd_x = lax.axis_index("gx") % 2 == 1
    even = even_ref[...] + even_in_ref[...]
    column = lax.axis_index("gx")
    at_end = (column == 0) | (column == lax.axis_size("gx") - 1)
    odd = odd_ref[...] + jnp.where(at_end, 0.0, odd_in_ref[...])
    left = jnp.where(odd_x, even, odd)
    right = jnp.where(odd_x, odd, even)
    edge = unpacked(left[half:, :]) + pltpu.roll(unpacked(right[half:, :]), 32, 1)
    lane = lax.broadcasted_iota(jnp.int32, (ROWS, 128), 1)
    edge_means, edge_table = table(edge)
    start = GROUPS * half
    full_ref[start:, 128:] = jnp.zeros((half, 128), f32)
    high, low = split(jnp.where(lane < 64, edge_table, 0.0))
    full_ref[start : start + ROWS, 0:128] = high
    full_ref[start + ROWS :, 0:128] = low
    high, low = split(edge_means)
    edge_means = jnp.where(lane < 64, high, pltpu.roll(low, 64, 1)).astype(bf16)
    row = lax.broadcasted_iota(jnp.int32, (128, CY), 0) & 63
    col = lax.broadcasted_iota(jnp.int32, (1, CY), 1)
    inner = (lane >= R) & (lane < CY - R)
    for group in range(GROUPS):
        source = left if group < 2 else right
        start = (group % 2) * ROWS
        means, cells = table(source[start : start + ROWS])
        high, low = split(cells)
        full_ref[group * half : group * half + ROWS, :] = high
        full_ref[group * half + ROWS : (group + 1) * half, :] = low
        if group in (1, 2):
            for odd_column in range(2):
                x = group * 2 + odd_column - R
                index = edge_index(jnp.full((1, CY), x + R, jnp.int32), col + R)
                placed = dot(edge_means, jnp.where(row == index, 1.0, 0.0).astype(bf16))
                own = jnp.where(inner, means[:, odd_column * CY : (odd_column + 1) * CY], placed)
                means_ref[:, x, :] = own[0:NSP]
    means_copy = pltpu.make_async_copy(means_ref, means_hbm, sems.at[0])
    means_copy.start()
    cells_ref[...] = full_ref[...].astype(bf16)
    mixed_ref[...] = jnp.zeros_like(mixed_ref)
    chunks = comp_ref.shape[1] // CHUNK

    def copy_of(chunk):
        at = pl.ds(chunk * CHUNK, CHUNK)
        return pltpu.make_async_copy(out_ref.at[:, at], updated_hbm.at[:, at], sems.at[1 + chunk])

    for chunk in range(chunks):
        at = pl.ds(chunk * CHUNK, CHUNK)
        gathered = dot(cells_ref[...], hot_ref[:, at])
        band = which_ref[0:1, at]
        chosen = gathered[0:half]
        for k in range(1, BANDS):
            chosen = jnp.where(band == k, gathered[k * half : (k + 1) * half], chosen)
        value = chosen[0:ROWS] + chosen[ROWS:]
        mixed_ref[0:NSP, :] = comp_ref[:, at] * value[NSP : NSP + 1] + value[0:NSP]
        level = which_ref[1:2, at]
        first, second = level == 0, level == 1
        z = dot(ops_ref[...], three(mixed_ref[...]))
        z = jnp.concatenate(
            [jnp.where(first, z[0:24], jnp.where(second, z[24:48], z[48:72])), z[72:104]], axis=0
        )
        source = jnp.concatenate([jnp.tanh(z), jnp.zeros((8, CHUNK), f32)], axis=0)
        z = dot(maps_ref[...], three(source))
        change = jnp.concatenate(
            [
                jnp.where(first, z[0:24], jnp.where(second, z[24:48], z[48:72])),
                jnp.where(level == 2, z[72:104], 0.0),
            ],
            axis=0,
        )
        out_ref[:, at] = mixed_ref[0:NSP, :] + change[0:NSP]
        copy_of(chunk).start()
    means_copy.wait()
    for chunk in range(chunks):
        copy_of(chunk).wait()


def swap(x, axis, odd):
    columns, rows = lax.axis_size("gx"), lax.axis_size("gy")

    def partner(i, j):
        at, count = (i, columns) if axis == "gx" else (j, rows)
        other = at + 1 if at % 2 == odd else at - 1
        if axis == "gx":
            return (other, j) if 0 <= other < count else (i, j ^ 1)
        return (i, other) if 0 <= other < count else (i ^ 1, j)

    pairs = []
    for i in range(columns):
        for j in range(rows):
            k, m = partner(i, j)
            pairs.append((i * rows + j, k * rows + m))
    return lax.ppermute(x, ("gx", "gy"), pairs)


def per_device(
    composition,
    particle_mass,
    particle_cell,
    particle_level,
    les_mean,
    mix_rate,
    rate_matrix,
    implicit_map,
):
    particles = composition.shape[1]
    sds = jax.ShapeDtypeStruct
    stay = lambda x: pltpu.with_memory_space_constraint(x, pltpu.HBM)
    hbm = pl.BlockSpec(memory_space=pltpu.HBM)
    vmem = pl.BlockSpec(memory_space=pltpu.VMEM)
    main, edge, local = pl.pallas_call(
        sums_kernel,
        out_shape=(
            sds((GROUPS * ROWS, 2 * CY), f32),
            sds((32, 128), f32),
            sds(composition.shape, f32),
        ),
        in_specs=[hbm] * 5,
        out_specs=(vmem,) * 3,
        scratch_shapes=[
            pltpu.VMEM(particle_mass.shape, f32),
            pltpu.VMEM(particle_cell.shape, jnp.int32),
            pltpu.VMEM(les_mean.shape, f32),
            pltpu.VMEM(mix_rate.shape, f32),
            pltpu.VMEM((ROWS, particles), f32),
            pltpu.VMEM((2 * CY, particles), bf16),
            pltpu.SemaphoreType.DMA((4 + pl.cdiv(NSP, ROWBLOCK),)),
        ],
        compiler_params=VMEM,
        name="cell_sums",
    )(*map(stay, (composition, particle_mass, particle_cell, les_mean, mix_rate)))
    edge_even = swap(edge, "gy", 0)
    edge_odd = swap(edge, "gy", 1)
    payload = sds((2 * ROWS + 8, 2 * CY), f32)
    odd, even = pl.pallas_call(
        pack_kernel,
        out_shape=(payload, payload),
        compiler_params=VMEM,
        name="pack",
    )(main, edge, edge_even, edge_odd)
    odd_in = swap(odd, "gx", 1)
    even_in = swap(even, "gx", 0)
    operator = sds((104, 192), bf16)
    places, which, ops, maps = pl.pallas_call(
        prepare_kernel,
        out_shape=(sds((2 * CY, particles), bf16), sds((2, particles), jnp.int32), operator, operator),
        in_specs=[vmem] * 4,
        out_specs=(vmem,) * 4,
        scratch_shapes=[pltpu.VMEM((104, 192), f32)],
        compiler_params=VMEM,
        cost_estimate=pl.CostEstimate(flops=1 << 22, bytes_accessed=8 << 20, transcendentals=0),
        name="prepare",
    )(particle_cell, particle_level, rate_matrix, implicit_map)
    return pl.pallas_call(
        react_kernel,
        out_shape=(sds(composition.shape, f32), sds(les_mean.shape, f32)),
        in_specs=[vmem] * 9,
        out_specs=(hbm, hbm),
        scratch_shapes=[
            pltpu.VMEM(les_mean.shape, f32),
            pltpu.VMEM((BANDS * 2 * ROWS, 2 * CY), f32),
            pltpu.VMEM((BANDS * 2 * ROWS, 2 * CY), bf16),
            pltpu.VMEM((64, CHUNK), f32),
            pltpu.VMEM(composition.shape, f32),
            pltpu.SemaphoreType.DMA((particles // CHUNK + 1,)),
        ],
        compiler_params=VMEM,
        name="gather_react",
    )(odd, even, odd_in, even_in, ops, maps, places, which, local)


def solution(mesh):
    placed = (
        P(None, ("gx", "gy")),
        P(("gx", "gy")),
        P(None, ("gx", "gy")),
        P(("gx", "gy")),
        P(None, "gx", "gy"),
        P("gx", "gy"),
        P(),
        P(),
    )
    return jax.shard_map(
        per_device,
        mesh=mesh,
        in_specs=placed,
        out_specs=(P(None, ("gx", "gy")), P(None, "gx", "gy")),
        check_vma=False,
    )
```

```python
import jax
import jax.numpy as jnp
from jax import lax
from jax.experimental import pallas as pl
from jax.experimental.pallas import tpu as pltpu
from jax.sharding import PartitionSpec as P

NS_LOW = 21
NS_MID = 24
NSP = 53
R = 2
CX = 4
CY = 128
ROWS = 56
GROUPS = 4
BANDS = GROUPS + 1
ROWBLOCK = 16
EDGE = 64
CHUNK = 4096
CHUNKS = (5120, 3072)
VMEM = pltpu.CompilerParams(vmem_limit_bytes=40 << 20)

prior_weight = 16.0
chem_step = 0.5

f32 = jnp.float32
bf16 = jnp.bfloat16


def split(x):
    high = x.astype(bf16).astype(f32)
    return high, x - high


def stacked(x):
    high, low = split(x)
    return jnp.concatenate([high, low], axis=0).astype(bf16)


def local_cells(cells):
    local_x = cells[0:1, :] - (lax.axis_index("gx") * CX - R)
    local_y = cells[1:2, :] - (lax.axis_index("gy") * CY - R)
    return local_x, local_y


def edge_index(local_x, local_y):
    place = jnp.where(local_y < 2 * R, local_y, local_y - CY + 16)
    return (local_x >> 2) * 32 + (local_x & 3) * 4 + place


def band_and_index(local_x, local_y):
    inside = (local_y >= 2 * R) & (local_y < CY)
    band = jnp.where(inside, local_x >> 1, GROUPS)
    index = jnp.where(inside, (local_x & 1) * CY + local_y - R, edge_index(local_x, local_y))
    return band, index


def hot(index, count):
    cells = lax.broadcasted_iota(jnp.int32, (count, index.shape[1]), 0)
    return jnp.where(cells == index, 1.0, 0.0).astype(bf16)


def hot_pair(index, count):
    cells = lax.broadcasted_iota(jnp.int32, (count, index.shape[1]), 0)
    return jnp.where((cells == index[0:1]) | (cells == index[1:2]), 1.0, 0.0).astype(bf16)


def dot_nt(a, b):
    return lax.dot_general(a, b, (((1,), (1,)), ((), ())), preferred_element_type=f32)


def dot(a, b):
    return jnp.dot(a, b, preferred_element_type=f32)


def own_cells(les_ref, rate_ref, cells_ref):
    cells_ref[NSP:, :] = jnp.zeros((ROWS - NSP, CX * CY), f32)
    for x in range(CX):
        at = slice(x * CY, (x + 1) * CY)
        cells_ref[0:NSP, at] = prior_weight * les_ref[:, x, :]
        cells_ref[NSP : NSP + 1, at] = jnp.full((1, CY), prior_weight, f32)
        cells_ref[NSP + 1 : NSP + 2, at] = rate_ref[x : x + 1, :]


def weighted(comp_ref, mass_ref, w_ref):
    particles = comp_ref.shape[1]
    mass = mass_ref[...].reshape(1, particles)
    w_ref[0:NSP, :] = comp_ref[...] * mass
    w_ref[NSP : NSP + 1, :] = mass
    w_ref[NSP + 1 :, :] = jnp.zeros((ROWS - NSP - 1, particles), f32)
    return stacked(w_ref[...])


def edge_kernel(
    comp_hbm, mass_hbm, cell_hbm, les_hbm, rate_hbm, edge_ref, comp_ref,
    mass_ref, cell_ref, les_ref, rate_ref, cells_ref, w_ref, sems,
):
    pairs = [(les_hbm, les_ref), (rate_hbm, rate_ref), (cell_hbm, cell_ref), (mass_hbm, mass_ref)]
    for start in range(0, NSP, ROWBLOCK):
        at = pl.ds(start, min(ROWBLOCK, NSP - start))
        pairs.append((comp_hbm.at[at], comp_ref.at[at]))
    copies = [pltpu.make_async_copy(src, dst, sems.at[i]) for i, (src, dst) in enumerate(pairs)]
    for copy in copies:
        copy.start()
    cells = CX * CY
    cell = lax.broadcasted_iota(jnp.int32, (1, cells), 1)
    band, index = band_and_index(cell // CY + R, cell % CY + R)
    place = hot(jnp.where(band == GROUPS, index, -1), EDGE)
    copies[0].wait()
    copies[1].wait()
    own_cells(les_ref, rate_ref, cells_ref)
    both = dot_nt(stacked(cells_ref[...]), place)
    for copy in copies[2:]:
        copy.wait()
    w = weighted(comp_ref, mass_ref, w_ref)
    band, index = band_and_index(*local_cells(cell_ref[...]))
    both += dot_nt(w, hot(jnp.where(band == GROUPS, index, -1), EDGE))
    edge = both[0:ROWS] + both[ROWS:]
    if EDGE < 128:
        edge = jnp.concatenate([edge, jnp.zeros((ROWS, 128 - EDGE), f32)], axis=1)
    lane = lax.broadcasted_iota(jnp.int32, (32, 128), 1)
    rest = pltpu.roll(jnp.concatenate([edge[32:], jnp.zeros((8, 128), f32)], axis=0), 64, 1)
    edge_ref[...] = jnp.where(lane < 64, edge[0:32], rest)


def main_kernel(comp_ref, mass_ref, cell_ref, les_ref, rate_ref, main_ref, cells_ref, w_ref):
    own_cells(les_ref, rate_ref, cells_ref)
    w = weighted(comp_ref, mass_ref, w_ref)
    band, index = band_and_index(*local_cells(cell_ref[...]))
    banded = [w * jnp.where(band == k, 1.0, 0.0).astype(bf16) for k in range(GROUPS)]
    both = dot_nt(jnp.concatenate(banded, axis=0), hot(index, 2 * CY))
    lane = lax.broadcasted_iota(jnp.int32, (ROWS, CY), 1)
    inner = (lane >= R) & (lane < CY - R)
    for k in range(GROUPS):
        start = 2 * ROWS * k
        sums = both[start : start + ROWS] + both[start + ROWS : start + 2 * ROWS]
        for odd in range(2):
            part = sums[:, odd * CY : (odd + 1) * CY]
            x = 2 * k + odd - R
            if 0 <= x < CX:
                part = part + jnp.where(inner, cells_ref[:, x * CY : (x + 1) * CY], 0.0)
            main_ref[k * ROWS : (k + 1) * ROWS, odd * CY : (odd + 1) * CY] = part


def pack_kernel(main_ref, edge_ref, even_in_ref, odd_in_ref, odd_ref, even_ref):
    odd_y = lax.axis_index("gy") % 2 == 1
    odd_x = lax.axis_index("gx") % 2 == 1
    even_in = even_in_ref[...]
    odd_in = odd_in_ref[...]
    row = lax.axis_index("gy")
    upper = jnp.where(row < lax.axis_size("gy") - 1, jnp.where(odd_y, odd_in, even_in), 0.0)
    lower = jnp.where(row > 0, jnp.where(odd_y, even_in, odd_in), 0.0)
    lane = lax.broadcasted_iota(jnp.int32, (32, 128), 1)
    high = (lane & 16) != 0
    both = edge_ref[...] + jnp.where(high, pltpu.roll(upper, 16, 1), pltpu.roll(lower, 112, 1))
    edge = jnp.concatenate([both, pltpu.roll(both, 64, 1)[0 : ROWS - 32]], axis=0)
    half = 2 * ROWS
    left, right = main_ref[0:half, :], main_ref[half:, :]
    even_ref[0:half, :] = jnp.where(odd_x, left, right)
    odd_ref[0:half, :] = jnp.where(odd_x, right, left)
    left_edge, right_edge = edge, pltpu.roll(edge, 96, 1)
    quarter = lane[0:8] >> 5
    for ref, part in (
        (even_ref, jnp.where(odd_x, left_edge, right_edge)),
        (odd_ref, jnp.where(odd_x, right_edge, left_edge)),
    ):
        for side in range(2):
            packed = jnp.zeros((8, 128), f32)
            for k in range(4):
                block = side * 4 + k
                if block < ROWS // 8:
                    rows = part[block * 8 : block * 8 + 8]
                    moved = pltpu.roll(rows, 32 * k, 1) if k else rows
                    packed = jnp.where(quarter == k, moved, packed)
            ref[half : half + 8, side * 128 : (side + 1) * 128] = packed


def table(total):
    rows = lax.broadcasted_iota(jnp.int32, total.shape, 0)
    mass = total[NSP : NSP + 1]
    mass = jnp.where(mass > 0.0, mass, 1.0)
    means = total / mass
    keep = jnp.exp(-total[NSP + 1 : NSP + 2])
    return means, jnp.where(rows < NSP, (1.0 - keep) * means, jnp.where(rows == NSP, keep, 0.0))


def unpacked(packed):
    lane = lax.broadcasted_iota(jnp.int32, (8, 128), 1)
    blocks = []
    for block in range(ROWS // 8):
        side, k = divmod(block, 4)
        rows = packed[:, side * 128 : (side + 1) * 128]
        rows = pltpu.roll(rows, 128 - 32 * k, 1) if k else rows
        blocks.append(jnp.where(lane < 32, rows, 0.0))
    return jnp.concatenate(blocks, axis=0)


def operator_rows(matrix_ref, full_ref, out_ref, scale):
    full_ref[...] = jnp.zeros_like(full_ref)
    start = 0
    for level, active in enumerate((NS_LOW, NS_MID, NSP)):
        rows = -(-active // 8) * 8
        count = min(rows, NSP)
        row = lax.broadcasted_iota(jnp.int32, (count, NSP), 0)
        col = lax.broadcasted_iota(jnp.int32, (count, NSP), 1)
        block = matrix_ref[level, 0:count, :] * scale
        high, low = split(jnp.where((row < active) & (col < active), block, 0.0))
        full_ref[start : start + count, 0:NSP] = high
        full_ref[start : start + count, 64 : 64 + NSP] = high
        full_ref[start : start + count, 128 : 128 + NSP] = low
        start += rows
    out_ref[...] = full_ref[...].astype(bf16)


def three(x):
    high = x.astype(bf16)
    low = (x - high.astype(f32)).astype(bf16)
    return jnp.concatenate([high, low, high], axis=0)


def prepare_kernel(cell_ref, level_ref, rate_ref, map_ref, hot_ref, which_ref, ops_ref, maps_ref, full_ref):
    operator_rows(rate_ref, full_ref, ops_ref, 1.0)
    operator_rows(map_ref, full_ref, maps_ref, chem_step)
    particles = cell_ref.shape[1]
    which_ref[1:2, :] = level_ref[...].reshape(1, particles)

    def body(i, carry):
        at = pl.ds(pl.multiple_of(i * CHUNK, CHUNK), CHUNK)
        band, index = band_and_index(*local_cells(cell_ref[:, at]))
        which_ref[0:1, at] = band
        index = jnp.concatenate([index, jnp.where(band == GROUPS, index + 64, index)], axis=0)
        hot_ref[:, at] = hot_pair(index, 2 * CY)
        return carry

    lax.fori_loop(0, particles // CHUNK, body, 0)


def react_kernel(
    odd_ref, even_ref, odd_in_ref, even_in_ref, ops_ref, maps_ref, hot_ref, which_ref, comp_ref,
    updated_hbm, means_hbm,
    means_ref, full_ref, cells_ref, mixed_ref, out_ref, sems,
):
    half = 2 * ROWS
    odd_x = lax.axis_index("gx") % 2 == 1
    even = even_ref[...] + even_in_ref[...]
    column = lax.axis_index("gx")
    at_end = (column == 0) | (column == lax.axis_size("gx") - 1)
    odd = odd_ref[...] + jnp.where(at_end, 0.0, odd_in_ref[...])
    left = jnp.where(odd_x, even, odd)
    right = jnp.where(odd_x, odd, even)
    edge = unpacked(left[half:, :]) + pltpu.roll(unpacked(right[half:, :]), 32, 1)
    lane = lax.broadcasted_iota(jnp.int32, (ROWS, 128), 1)
    edge_means, edge_table = table(edge)
    start = GROUPS * half
    full_ref[start:, 128:] = jnp.zeros((ROWS, 128), f32)
    high, low = split(edge_table)
    full_ref[start:, 0:128] = jnp.where(lane < 64, high, pltpu.roll(low, 64, 1))
    high, low = split(edge_means)
    edge_means = jnp.where(lane < 64, high, pltpu.roll(low, 64, 1)).astype(bf16)
    row = lax.broadcasted_iota(jnp.int32, (128, CY), 0) & 63
    col = lax.broadcasted_iota(jnp.int32, (1, CY), 1)
    inner = (lane >= R) & (lane < CY - R)
    for group in range(GROUPS):
        source = left if group < 2 else right
        start = (group % 2) * ROWS
        means, cells = table(source[start : start + ROWS])
        high, low = split(cells)
        full_ref[group * half : group * half + ROWS, :] = high
        full_ref[group * half + ROWS : (group + 1) * half, :] = low
        if group in (1, 2):
            for odd_column in range(2):
                x = group * 2 + odd_column - R
                index = edge_index(jnp.full((1, CY), x + R, jnp.int32), col + R)
                placed = dot(edge_means, jnp.where(row == index, 1.0, 0.0).astype(bf16))
                own = jnp.where(inner, means[:, odd_column * CY : (odd_column + 1) * CY], placed)
                means_ref[:, x, :] = own[0:NSP]
    means_copy = pltpu.make_async_copy(means_ref, means_hbm, sems.at[0])
    means_copy.start()
    cells_ref[...] = full_ref[...].astype(bf16)
    mixed_ref[...] = jnp.zeros_like(mixed_ref)
    chunks = len(CHUNKS)

    def copy_of(chunk):
        at = pl.ds(sum(CHUNKS[:chunk]), CHUNKS[chunk])
        return pltpu.make_async_copy(out_ref.at[:, at], updated_hbm.at[:, at], sems.at[1 + chunk])

    for chunk in range(chunks):
        width = CHUNKS[chunk]
        at = pl.ds(sum(CHUNKS[:chunk]), width)
        gathered = dot(cells_ref[...], hot_ref[:, at])
        band = which_ref[0:1, at]
        chosen = gathered[0:half]
        for k in range(1, GROUPS):
            chosen = jnp.where(band == k, gathered[k * half : (k + 1) * half], chosen)
        value = jnp.where(band == GROUPS, gathered[GROUPS * half :], chosen[0:ROWS] + chosen[ROWS:])
        mixed_ref[0:NSP, 0:width] = comp_ref[:, at] * value[NSP : NSP + 1] + value[0:NSP]
        level = which_ref[1:2, at]
        first, second = level == 0, level == 1
        z = dot(ops_ref[...], three(mixed_ref[:, 0:width]))
        z = jnp.concatenate(
            [jnp.where(first, z[0:24], jnp.where(second, z[24:48], z[48:72])), z[72:104]], axis=0
        )
        source = jnp.concatenate([jnp.tanh(z), jnp.zeros((8, width), f32)], axis=0)
        z = dot(maps_ref[...], three(source))
        change = jnp.concatenate(
            [
                jnp.where(first, z[0:24], jnp.where(second, z[24:48], z[48:72])),
                jnp.where(level == 2, z[72:104], 0.0),
            ],
            axis=0,
        )
        out_ref[:, at] = mixed_ref[0:NSP, 0:width] + change[0:NSP]
        copy_of(chunk).start()
    means_copy.wait()
    for chunk in range(chunks):
        copy_of(chunk).wait()


def swap(x, axis, odd):
    columns, rows = lax.axis_size("gx"), lax.axis_size("gy")

    def partner(i, j):
        at, count = (i, columns) if axis == "gx" else (j, rows)
        other = at + 1 if at % 2 == odd else at - 1
        if axis == "gx":
            return (other, j) if 0 <= other < count else (i, j ^ 1)
        return (i, other) if 0 <= other < count else (i ^ 1, j)

    pairs = []
    for i in range(columns):
        for j in range(rows):
            k, m = partner(i, j)
            pairs.append((i * rows + j, k * rows + m))
    return lax.ppermute(x, ("gx", "gy"), pairs)


def per_device(
    composition,
    particle_mass,
    particle_cell,
    particle_level,
    les_mean,
    mix_rate,
    rate_matrix,
    implicit_map,
):
    particles = composition.shape[1]
    sds = jax.ShapeDtypeStruct
    stay = lambda x: pltpu.with_memory_space_constraint(x, pltpu.HBM)
    hbm = pl.BlockSpec(memory_space=pltpu.HBM)
    vmem = pl.BlockSpec(memory_space=pltpu.VMEM)
    prior = pltpu.VMEM((ROWS, CX * CY), f32)
    edge, local = pl.pallas_call(
        edge_kernel,
        out_shape=(sds((32, 128), f32), sds(composition.shape, f32)),
        in_specs=[hbm] * 5,
        out_specs=(vmem, vmem),
        scratch_shapes=[
            pltpu.VMEM(particle_mass.shape, f32),
            pltpu.VMEM(particle_cell.shape, jnp.int32),
            pltpu.VMEM(les_mean.shape, f32),
            pltpu.VMEM(mix_rate.shape, f32),
            prior,
            pltpu.VMEM((ROWS, particles), f32),
            pltpu.SemaphoreType.DMA((4 + pl.cdiv(NSP, ROWBLOCK),)),
        ],
        compiler_params=VMEM,
        name="edge_sums",
    )(*map(stay, (composition, particle_mass, particle_cell, les_mean, mix_rate)))
    main = pl.pallas_call(
        main_kernel,
        out_shape=sds((GROUPS * ROWS, 2 * CY), f32),
        in_specs=[vmem] * 5,
        out_specs=vmem,
        scratch_shapes=[prior, pltpu.VMEM((ROWS, particles), f32)],
        compiler_params=VMEM,
        cost_estimate=pl.CostEstimate(flops=1 << 32, bytes_accessed=8 << 20, transcendentals=0),
        name="cell_sums",
    )(local, particle_mass, particle_cell, les_mean, mix_rate)
    edge_even = swap(edge, "gy", 0)
    edge_odd = swap(edge, "gy", 1)
    payload = sds((2 * ROWS + 8, 2 * CY), f32)
    odd, even = pl.pallas_call(
        pack_kernel,
        out_shape=(payload, payload),
        compiler_params=VMEM,
        name="pack",
    )(main, edge, edge_even, edge_odd)
    odd_in = swap(odd, "gx", 1)
    even_in = swap(even, "gx", 0)
    operator = sds((104, 192), bf16)
    places, which, ops, maps = pl.pallas_call(
        prepare_kernel,
        out_shape=(sds((2 * CY, particles), bf16), sds((2, particles), jnp.int32), operator, operator),
        in_specs=[vmem] * 4,
        out_specs=(vmem,) * 4,
        scratch_shapes=[pltpu.VMEM((104, 192), f32)],
        compiler_params=VMEM,
        cost_estimate=pl.CostEstimate(flops=1 << 22, bytes_accessed=8 << 20, transcendentals=0),
        name="prepare",
    )(particle_cell, particle_level, rate_matrix, implicit_map)
    return pl.pallas_call(
        react_kernel,
        out_shape=(sds(composition.shape, f32), sds(les_mean.shape, f32)),
        in_specs=[vmem] * 9,
        out_specs=(hbm, hbm),
        scratch_shapes=[
            pltpu.VMEM(les_mean.shape, f32),
            pltpu.VMEM(((BANDS + GROUPS) * ROWS, 2 * CY), f32),
            pltpu.VMEM(((BANDS + GROUPS) * ROWS, 2 * CY), bf16),
            pltpu.VMEM((64, max(CHUNKS)), f32),
            pltpu.VMEM(composition.shape, f32),
            pltpu.SemaphoreType.DMA((len(CHUNKS) + 1,)),
        ],
        compiler_params=VMEM,
        name="gather_react",
    )(odd, even, odd_in, even_in, ops, maps, places, which, local)


def solution(mesh):
    placed = (
        P(None, ("gx", "gy")),
        P(("gx", "gy")),
        P(None, ("gx", "gy")),
        P(("gx", "gy")),
        P(None, "gx", "gy"),
        P("gx", "gy"),
        P(),
        P(),
    )
    return jax.shard_map(
        per_device,
        mesh=mesh,
        in_specs=placed,
        out_specs=(P(None, ("gx", "gy")), P(None, "gx", "gy")),
        check_vma=False,
    )
```

```python
import jax
import jax.numpy as jnp
from jax import lax
from jax.experimental import pallas as pl
from jax.experimental.pallas import tpu as pltpu
from jax.sharding import PartitionSpec as P

NS_LOW = 21
NS_MID = 24
NSP = 53
R = 2
CX = 4
CY = 128
ROWS = 56
GROUPS = 4
BANDS = GROUPS + 1
ROWBLOCK = 16
EDGE = 64
WIDTH = 4096
CHUNK = 4096
CHUNKS = (5120, 3072)
STRETCHES = ((5120,), (1536, 1536))
VMEM = pltpu.CompilerParams(vmem_limit_bytes=40 << 20)

prior_weight = 16.0
chem_step = 0.5

f32 = jnp.float32
bf16 = jnp.bfloat16


def split(x):
    high = x.astype(bf16).astype(f32)
    return high, x - high


def stacked(x):
    high, low = split(x)
    return jnp.concatenate([high, low], axis=0).astype(bf16)


def local_cells(cells):
    local_x = cells[0:1, :] - (lax.axis_index("gx") * CX - R)
    local_y = cells[1:2, :] - (lax.axis_index("gy") * CY - R)
    return local_x, local_y


def edge_index(local_x, local_y):
    place = jnp.where(local_y < 2 * R, local_y, local_y - CY + 16)
    return (local_x >> 2) * 32 + (local_x & 3) * 4 + place


def band_and_index(local_x, local_y):
    inside = (local_y >= 2 * R) & (local_y < CY)
    band = jnp.where(inside, local_x >> 1, GROUPS)
    index = jnp.where(inside, (local_x & 1) * CY + local_y - R, edge_index(local_x, local_y))
    return band, index


def hot(index, count):
    cells = lax.broadcasted_iota(jnp.int32, (count, index.shape[1]), 0)
    return jnp.where(cells == index, 1.0, 0.0).astype(bf16)


def hot_pair(index, count):
    cells = lax.broadcasted_iota(jnp.int32, (count, index.shape[1]), 0)
    return jnp.where((cells == index[0:1]) | (cells == index[1:2]), 1.0, 0.0).astype(bf16)


def dot_nt(a, b):
    return lax.dot_general(a, b, (((1,), (1,)), ((), ())), preferred_element_type=f32)


def dot(a, b):
    return jnp.dot(a, b, preferred_element_type=f32)


def own_cells(les_ref, rate_ref, cells_ref):
    cells_ref[NSP:, :] = jnp.zeros((ROWS - NSP, CX * CY), f32)
    for x in range(CX):
        at = slice(x * CY, (x + 1) * CY)
        cells_ref[0:NSP, at] = prior_weight * les_ref[:, x, :]
        cells_ref[NSP : NSP + 1, at] = jnp.full((1, CY), prior_weight, f32)
        cells_ref[NSP + 1 : NSP + 2, at] = rate_ref[x : x + 1, :]


def weighted(comp_ref, mass_ref, w_ref):
    particles = comp_ref.shape[1]
    mass = mass_ref[...].reshape(1, particles)
    w_ref[0:NSP, :] = comp_ref[...] * mass
    w_ref[NSP : NSP + 1, :] = mass
    w_ref[NSP + 1 :, :] = jnp.zeros((ROWS - NSP - 1, particles), f32)
    return stacked(w_ref[...])


def edge_kernel(
    comp_hbm, mass_hbm, cell_hbm, les_hbm, rate_hbm, edge_ref, comp_ref,
    mass_ref, cell_ref, les_ref, rate_ref, cells_ref, w_ref, sems,
):
    pairs = [(les_hbm, les_ref), (rate_hbm, rate_ref), (cell_hbm, cell_ref), (mass_hbm, mass_ref)]
    small = len(pairs)
    for start in range(0, comp_ref.shape[1], WIDTH):
        at = pl.ds(start, WIDTH)
        pairs.append((comp_hbm.at[:, at], comp_ref.at[:, at]))
    copies = [pltpu.make_async_copy(src, dst, sems.at[i]) for i, (src, dst) in enumerate(pairs)]
    for copy in copies:
        copy.start()
    cells = CX * CY
    cell = lax.broadcasted_iota(jnp.int32, (1, cells), 1)
    band, index = band_and_index(cell // CY + R, cell % CY + R)
    place = hot(jnp.where(band == GROUPS, index, -1), EDGE)
    copies[0].wait()
    copies[1].wait()
    own_cells(les_ref, rate_ref, cells_ref)
    both = dot_nt(stacked(cells_ref[...]), place)
    for copy in copies[2:small]:
        copy.wait()
    w_ref[NSP + 1 :, :] = jnp.zeros((ROWS - NSP - 1, WIDTH), f32)

    def body(i, total):
        at = pl.ds(pl.multiple_of(i * WIDTH, WIDTH), WIDTH)
        pltpu.make_async_copy(comp_hbm.at[:, at], comp_ref.at[:, at], sems.at[small + i]).wait()
        mass = mass_ref[at].reshape(1, WIDTH)
        w_ref[0:NSP, :] = comp_ref[:, at] * mass
        w_ref[NSP : NSP + 1, :] = mass
        band, index = band_and_index(*local_cells(cell_ref[:, at]))
        place = hot(jnp.where(band == GROUPS, index, -1), EDGE)
        return total + dot_nt(stacked(w_ref[...]), place)

    both = lax.fori_loop(0, comp_ref.shape[1] // WIDTH, body, both)
    edge = both[0:ROWS] + both[ROWS:]
    if EDGE < 128:
        edge = jnp.concatenate([edge, jnp.zeros((ROWS, 128 - EDGE), f32)], axis=1)
    lane = lax.broadcasted_iota(jnp.int32, (32, 128), 1)
    rest = pltpu.roll(jnp.concatenate([edge[32:], jnp.zeros((8, 128), f32)], axis=0), 64, 1)
    edge_ref[...] = jnp.where(lane < 64, edge[0:32], rest)


def main_kernel(comp_ref, mass_ref, cell_ref, les_ref, rate_ref, main_ref, cells_ref, w_ref):
    own_cells(les_ref, rate_ref, cells_ref)
    w = weighted(comp_ref, mass_ref, w_ref)
    band, index = band_and_index(*local_cells(cell_ref[...]))
    banded = [w * jnp.where(band == k, 1.0, 0.0).astype(bf16) for k in range(GROUPS)]
    both = dot_nt(jnp.concatenate(banded, axis=0), hot(index, 2 * CY))
    lane = lax.broadcasted_iota(jnp.int32, (ROWS, CY), 1)
    inner = (lane >= R) & (lane < CY - R)
    for k in range(GROUPS):
        start = 2 * ROWS * k
        sums = both[start : start + ROWS] + both[start + ROWS : start + 2 * ROWS]
        for odd in range(2):
            part = sums[:, odd * CY : (odd + 1) * CY]
            x = 2 * k + odd - R
            if 0 <= x < CX:
                part = part + jnp.where(inner, cells_ref[:, x * CY : (x + 1) * CY], 0.0)
            main_ref[k * ROWS : (k + 1) * ROWS, odd * CY : (odd + 1) * CY] = part


def pack_kernel(main_ref, edge_ref, even_in_ref, odd_in_ref, odd_ref, even_ref):
    odd_y = lax.axis_index("gy") % 2 == 1
    odd_x = lax.axis_index("gx") % 2 == 1
    even_in = even_in_ref[...]
    odd_in = odd_in_ref[...]
    row = lax.axis_index("gy")
    upper = jnp.where(row < lax.axis_size("gy") - 1, jnp.where(odd_y, odd_in, even_in), 0.0)
    lower = jnp.where(row > 0, jnp.where(odd_y, even_in, odd_in), 0.0)
    lane = lax.broadcasted_iota(jnp.int32, (32, 128), 1)
    high = (lane & 16) != 0
    both = edge_ref[...] + jnp.where(high, pltpu.roll(upper, 16, 1), pltpu.roll(lower, 112, 1))
    edge = jnp.concatenate([both, pltpu.roll(both, 64, 1)[0 : ROWS - 32]], axis=0)
    half = 2 * ROWS
    left, right = main_ref[0:half, :], main_ref[half:, :]
    even_ref[0:half, :] = jnp.where(odd_x, left, right)
    odd_ref[0:half, :] = jnp.where(odd_x, right, left)
    left_edge, right_edge = edge, pltpu.roll(edge, 96, 1)
    quarter = lane[0:8] >> 5
    for ref, part in (
        (even_ref, jnp.where(odd_x, left_edge, right_edge)),
        (odd_ref, jnp.where(odd_x, right_edge, left_edge)),
    ):
        for side in range(2):
            packed = jnp.zeros((8, 128), f32)
            for k in range(4):
                block = side * 4 + k
                if block < ROWS // 8:
                    rows = part[block * 8 : block * 8 + 8]
                    moved = pltpu.roll(rows, 32 * k, 1) if k else rows
                    packed = jnp.where(quarter == k, moved, packed)
            ref[half : half + 8, side * 128 : (side + 1) * 128] = packed


def table(total):
    rows = lax.broadcasted_iota(jnp.int32, total.shape, 0)
    mass = total[NSP : NSP + 1]
    mass = jnp.where(mass > 0.0, mass, 1.0)
    means = total / mass
    keep = jnp.exp(-total[NSP + 1 : NSP + 2])
    return means, jnp.where(rows < NSP, (1.0 - keep) * means, jnp.where(rows == NSP, keep, 0.0))


def unpacked(packed):
    lane = lax.broadcasted_iota(jnp.int32, (8, 128), 1)
    blocks = []
    for block in range(ROWS // 8):
        side, k = divmod(block, 4)
        rows = packed[:, side * 128 : (side + 1) * 128]
        rows = pltpu.roll(rows, 128 - 32 * k, 1) if k else rows
        blocks.append(jnp.where(lane < 32, rows, 0.0))
    return jnp.concatenate(blocks, axis=0)


def operator_rows(matrix_ref, full_ref, out_ref, scale):
    full_ref[...] = jnp.zeros_like(full_ref)
    start = 0
    for level, active in enumerate((NS_LOW, NS_MID, NSP)):
        rows = -(-active // 8) * 8
        count = min(rows, NSP)
        row = lax.broadcasted_iota(jnp.int32, (count, NSP), 0)
        col = lax.broadcasted_iota(jnp.int32, (count, NSP), 1)
        block = matrix_ref[level, 0:count, :] * scale
        high, low = split(jnp.where((row < active) & (col < active), block, 0.0))
        full_ref[start : start + count, 0:NSP] = high
        full_ref[start : start + count, 64 : 64 + NSP] = high
        full_ref[start : start + count, 128 : 128 + NSP] = low
        start += rows
    out_ref[...] = full_ref[...].astype(bf16)


def three(x):
    high = x.astype(bf16)
    low = (x - high.astype(f32)).astype(bf16)
    return jnp.concatenate([high, low, high], axis=0)


def prepare_kernel(cell_ref, level_ref, rate_ref, map_ref, hot_ref, which_ref, ops_ref, maps_ref, full_ref):
    operator_rows(rate_ref, full_ref, ops_ref, 1.0)
    operator_rows(map_ref, full_ref, maps_ref, chem_step)
    particles = cell_ref.shape[1]
    which_ref[1:2, :] = level_ref[...].reshape(1, particles)

    def body(i, carry):
        at = pl.ds(pl.multiple_of(i * CHUNK, CHUNK), CHUNK)
        band, index = band_and_index(*local_cells(cell_ref[:, at]))
        which_ref[0:1, at] = band
        index = jnp.concatenate([index, jnp.where(band == GROUPS, index + 64, index)], axis=0)
        hot_ref[:, at] = hot_pair(index, 2 * CY)
        return carry

    lax.fori_loop(0, particles // CHUNK, body, 0)


def react_kernel(
    odd_ref, even_ref, odd_in_ref, even_in_ref, ops_ref, maps_ref, hot_ref, which_ref, comp_ref,
    updated_hbm, means_hbm,
    means_ref, full_ref, cells_ref, mixed_ref, out_ref, sems,
):
    half = 2 * ROWS
    odd_x = lax.axis_index("gx") % 2 == 1
    even = even_ref[...] + even_in_ref[...]
    column = lax.axis_index("gx")
    at_end = (column == 0) | (column == lax.axis_size("gx") - 1)
    odd = odd_ref[...] + jnp.where(at_end, 0.0, odd_in_ref[...])
    left = jnp.where(odd_x, even, odd)
    right = jnp.where(odd_x, odd, even)
    edge = unpacked(left[half:, :]) + pltpu.roll(unpacked(right[half:, :]), 32, 1)
    lane = lax.broadcasted_iota(jnp.int32, (ROWS, 128), 1)
    edge_means, edge_table = table(edge)
    start = GROUPS * half
    full_ref[start:, 128:] = jnp.zeros((ROWS, 128), f32)
    high, low = split(edge_table)
    full_ref[start:, 0:128] = jnp.where(lane < 64, high, pltpu.roll(low, 64, 1))
    high, low = split(edge_means)
    edge_means = jnp.where(lane < 64, high, pltpu.roll(low, 64, 1)).astype(bf16)
    row = lax.broadcasted_iota(jnp.int32, (128, CY), 0) & 63
    col = lax.broadcasted_iota(jnp.int32, (1, CY), 1)
    inner = (lane >= R) & (lane < CY - R)
    for group in range(GROUPS):
        source = left if group < 2 else right
        start = (group % 2) * ROWS
        means, cells = table(source[start : start + ROWS])
        high, low = split(cells)
        full_ref[group * half : group * half + ROWS, :] = high
        full_ref[group * half + ROWS : (group + 1) * half, :] = low
        if group in (1, 2):
            for odd_column in range(2):
                x = group * 2 + odd_column - R
                index = edge_index(jnp.full((1, CY), x + R, jnp.int32), col + R)
                placed = dot(edge_means, jnp.where(row == index, 1.0, 0.0).astype(bf16))
                own = jnp.where(inner, means[:, odd_column * CY : (odd_column + 1) * CY], placed)
                means_ref[:, x, :] = own[0:NSP]
    means_copy = pltpu.make_async_copy(means_ref, means_hbm, sems.at[0])
    means_copy.start()
    cells_ref[...] = full_ref[...].astype(bf16)
    mixed_ref[...] = jnp.zeros_like(mixed_ref)
    chunks = len(CHUNKS)
    sent = []

    for chunk in range(chunks):
        width = CHUNKS[chunk]
        at = pl.ds(sum(CHUNKS[:chunk]), width)
        gathered = dot(cells_ref[...], hot_ref[:, at])
        band = which_ref[0:1, at]
        chosen = gathered[0:half]
        for k in range(1, GROUPS):
            chosen = jnp.where(band == k, gathered[k * half : (k + 1) * half], chosen)
        value = jnp.where(band == GROUPS, gathered[GROUPS * half :], chosen[0:ROWS] + chosen[ROWS:])
        mixed_ref[0:NSP, 0:width] = comp_ref[:, at] * value[NSP : NSP + 1] + value[0:NSP]
        level = which_ref[1:2, at]
        first, second = level == 0, level == 1
        z = dot(ops_ref[...], three(mixed_ref[:, 0:width]))
        z = jnp.concatenate(
            [jnp.where(first, z[0:24], jnp.where(second, z[24:48], z[48:72])), z[72:104]], axis=0
        )
        source = jnp.concatenate([jnp.tanh(z), jnp.zeros((8, width), f32)], axis=0)
        parts = three(source)
        begin = 0
        for stretch in STRETCHES[chunk]:
            inside = slice(begin, begin + stretch)
            z = dot(maps_ref[...], parts[:, inside])
            one, two = first[:, inside], second[:, inside]
            change = jnp.concatenate(
                [
                    jnp.where(one, z[0:24], jnp.where(two, z[24:48], z[48:72])),
                    jnp.where(level[:, inside] == 2, z[72:104], 0.0),
                ],
                axis=0,
            )
            columns = pl.ds(sum(CHUNKS[:chunk]) + begin, stretch)
            out_ref[:, columns] = mixed_ref[0:NSP, inside] + change[0:NSP]
            out = pltpu.make_async_copy(
                out_ref.at[:, columns], updated_hbm.at[:, columns], sems.at[1 + len(sent)]
            )
            out.start()
            sent.append(out)
            begin += stretch
    means_copy.wait()
    for out in sent:
        out.wait()


def swap(x, axis, odd):
    columns, rows = lax.axis_size("gx"), lax.axis_size("gy")

    def partner(i, j):
        at, count = (i, columns) if axis == "gx" else (j, rows)
        other = at + 1 if at % 2 == odd else at - 1
        if axis == "gx":
            return (other, j) if 0 <= other < count else (i, j ^ 1)
        return (i, other) if 0 <= other < count else (i ^ 1, j)

    pairs = []
    for i in range(columns):
        for j in range(rows):
            k, m = partner(i, j)
            pairs.append((i * rows + j, k * rows + m))
    return lax.ppermute(x, ("gx", "gy"), pairs)


def per_device(
    composition,
    particle_mass,
    particle_cell,
    particle_level,
    les_mean,
    mix_rate,
    rate_matrix,
    implicit_map,
):
    particles = composition.shape[1]
    sds = jax.ShapeDtypeStruct
    stay = lambda x: pltpu.with_memory_space_constraint(x, pltpu.HBM)
    hbm = pl.BlockSpec(memory_space=pltpu.HBM)
    vmem = pl.BlockSpec(memory_space=pltpu.VMEM)
    prior = pltpu.VMEM((ROWS, CX * CY), f32)
    edge, local = pl.pallas_call(
        edge_kernel,
        out_shape=(sds((32, 128), f32), sds(composition.shape, f32)),
        in_specs=[hbm] * 5,
        out_specs=(vmem, vmem),
        scratch_shapes=[
            pltpu.VMEM(particle_mass.shape, f32),
            pltpu.VMEM(particle_cell.shape, jnp.int32),
            pltpu.VMEM(les_mean.shape, f32),
            pltpu.VMEM(mix_rate.shape, f32),
            prior,
            pltpu.VMEM((ROWS, WIDTH), f32),
            pltpu.SemaphoreType.DMA((4 + particles // WIDTH,)),
        ],
        compiler_params=VMEM,
        name="edge_sums",
    )(*map(stay, (composition, particle_mass, particle_cell, les_mean, mix_rate)))
    main = pl.pallas_call(
        main_kernel,
        out_shape=sds((GROUPS * ROWS, 2 * CY), f32),
        in_specs=[vmem] * 5,
        out_specs=vmem,
        scratch_shapes=[prior, pltpu.VMEM((ROWS, particles), f32)],
        compiler_params=VMEM,
        cost_estimate=pl.CostEstimate(flops=1 << 32, bytes_accessed=8 << 20, transcendentals=0),
        name="cell_sums",
    )(local, particle_mass, particle_cell, les_mean, mix_rate)
    edge_even = swap(edge, "gy", 0)
    edge_odd = swap(edge, "gy", 1)
    payload = sds((2 * ROWS + 8, 2 * CY), f32)
    odd, even = pl.pallas_call(
        pack_kernel,
        out_shape=(payload, payload),
        compiler_params=VMEM,
        name="pack",
    )(main, edge, edge_even, edge_odd)
    odd_in = swap(odd, "gx", 1)
    even_in = swap(even, "gx", 0)
    operator = sds((104, 192), bf16)
    places, which, ops, maps = pl.pallas_call(
        prepare_kernel,
        out_shape=(sds((2 * CY, particles), bf16), sds((2, particles), jnp.int32), operator, operator),
        in_specs=[vmem] * 4,
        out_specs=(vmem,) * 4,
        scratch_shapes=[pltpu.VMEM((104, 192), f32)],
        compiler_params=VMEM,
        cost_estimate=pl.CostEstimate(flops=1 << 22, bytes_accessed=8 << 20, transcendentals=0),
        name="prepare",
    )(particle_cell, particle_level, rate_matrix, implicit_map)
    return pl.pallas_call(
        react_kernel,
        out_shape=(sds(composition.shape, f32), sds(les_mean.shape, f32)),
        in_specs=[vmem] * 9,
        out_specs=(hbm, hbm),
        scratch_shapes=[
            pltpu.VMEM(les_mean.shape, f32),
            pltpu.VMEM(((BANDS + GROUPS) * ROWS, 2 * CY), f32),
            pltpu.VMEM(((BANDS + GROUPS) * ROWS, 2 * CY), bf16),
            pltpu.VMEM((64, max(CHUNKS)), f32),
            pltpu.VMEM(composition.shape, f32),
            pltpu.SemaphoreType.DMA((sum(map(len, STRETCHES)) + 1,)),
        ],
        compiler_params=VMEM,
        name="gather_react",
    )(odd, even, odd_in, even_in, ops, maps, places, which, local)


def solution(mesh):
    placed = (
        P(None, ("gx", "gy")),
        P(("gx", "gy")),
        P(None, ("gx", "gy")),
        P(("gx", "gy")),
        P(None, "gx", "gy"),
        P("gx", "gy"),
        P(),
        P(),
    )
    return jax.shard_map(
        per_device,
        mesh=mesh,
        in_specs=placed,
        out_specs=(P(None, ("gx", "gy")), P(None, "gx", "gy")),
        check_vma=False,
    )
```

```python
import jax
import jax.numpy as jnp
from jax import lax
from jax.experimental import pallas as pl
from jax.experimental.pallas import tpu as pltpu
from jax.sharding import PartitionSpec as P

NS_LOW = 21
NS_MID = 24
NSP = 53
R = 2
CX = 4
CY = 128
ROWS = 56
GROUPS = 4
BANDS = GROUPS + 1
ROWBLOCK = 16
EDGE = 64
WIDTH = 4096
CHUNK = 4096
CHUNKS = (5120, 3072)
STRETCHES = ((5120,), (1536, 1536))
VMEM = pltpu.CompilerParams(vmem_limit_bytes=40 << 20)

prior_weight = 16.0
chem_step = 0.5

f32 = jnp.float32
bf16 = jnp.bfloat16


def split(x):
    high = x.astype(bf16).astype(f32)
    return high, x - high


def stacked(x):
    high, low = split(x)
    return jnp.concatenate([high, low], axis=0).astype(bf16)


def local_cells(cells):
    local_x = cells[0:1, :] - (lax.axis_index("gx") * CX - R)
    local_y = cells[1:2, :] - (lax.axis_index("gy") * CY - R)
    return local_x, local_y


def edge_index(local_x, local_y):
    place = jnp.where(local_y < 2 * R, local_y, local_y - CY + 16)
    return (local_x >> 2) * 32 + (local_x & 3) * 4 + place


def band_and_index(local_x, local_y):
    inside = (local_y >= 2 * R) & (local_y < CY)
    band = jnp.where(inside, local_x >> 1, GROUPS)
    index = jnp.where(inside, (local_x & 1) * CY + local_y - R, edge_index(local_x, local_y))
    return band, index


def hot(index, count):
    cells = lax.broadcasted_iota(jnp.int32, (count, index.shape[1]), 0)
    return jnp.where(cells == index, 1.0, 0.0).astype(bf16)


def hot_pair(index, count):
    cells = lax.broadcasted_iota(jnp.int32, (count, index.shape[1]), 0)
    return jnp.where((cells == index[0:1]) | (cells == index[1:2]), 1.0, 0.0).astype(bf16)


def dot_nt(a, b):
    return lax.dot_general(a, b, (((1,), (1,)), ((), ())), preferred_element_type=f32)


def dot(a, b):
    return jnp.dot(a, b, preferred_element_type=f32)


def own_cells(les_ref, rate_ref, cells_ref):
    cells_ref[NSP:, :] = jnp.zeros((ROWS - NSP, CX * CY), f32)
    for x in range(CX):
        at = slice(x * CY, (x + 1) * CY)
        cells_ref[0:NSP, at] = prior_weight * les_ref[:, x, :]
        cells_ref[NSP : NSP + 1, at] = jnp.full((1, CY), prior_weight, f32)
        cells_ref[NSP + 1 : NSP + 2, at] = rate_ref[x : x + 1, :]


def weighted(comp_ref, mass_ref, w_ref):
    particles = comp_ref.shape[1]
    mass = mass_ref[...].reshape(1, particles)
    w_ref[0:NSP, :] = comp_ref[...] * mass
    w_ref[NSP : NSP + 1, :] = mass
    w_ref[NSP + 1 :, :] = jnp.zeros((ROWS - NSP - 1, particles), f32)
    return stacked(w_ref[...])


def edge_kernel(
    comp_hbm, mass_hbm, cell_hbm, les_hbm, rate_hbm, edge_ref, comp_ref,
    mass_ref, cell_ref, les_ref, rate_ref, cells_ref, w_ref, sems,
):
    pairs = [(les_hbm, les_ref), (rate_hbm, rate_ref), (cell_hbm, cell_ref), (mass_hbm, mass_ref)]
    small = len(pairs)
    for start in range(0, comp_ref.shape[1], WIDTH):
        at = pl.ds(start, WIDTH)
        pairs.append((comp_hbm.at[:, at], comp_ref.at[:, at]))
    copies = [pltpu.make_async_copy(src, dst, sems.at[i]) for i, (src, dst) in enumerate(pairs)]
    for copy in copies:
        copy.start()
    cells = CX * CY
    cell = lax.broadcasted_iota(jnp.int32, (1, cells), 1)
    band, index = band_and_index(cell // CY + R, cell % CY + R)
    place = hot(jnp.where(band == GROUPS, index, -1), EDGE)
    copies[0].wait()
    copies[1].wait()
    own_cells(les_ref, rate_ref, cells_ref)
    both = dot_nt(stacked(cells_ref[...]), place)
    for copy in copies[2:small]:
        copy.wait()
    w_ref[NSP + 1 :, :] = jnp.zeros((ROWS - NSP - 1, WIDTH), f32)

    def body(i, total):
        at = pl.ds(pl.multiple_of(i * WIDTH, WIDTH), WIDTH)
        pltpu.make_async_copy(comp_hbm.at[:, at], comp_ref.at[:, at], sems.at[small + i]).wait()
        mass = mass_ref[at].reshape(1, WIDTH)
        w_ref[0:NSP, :] = comp_ref[:, at] * mass
        w_ref[NSP : NSP + 1, :] = mass
        band, index = band_and_index(*local_cells(cell_ref[:, at]))
        place = hot(jnp.where(band == GROUPS, index, -1), EDGE)
        return total + dot_nt(stacked(w_ref[...]), place)

    both = lax.fori_loop(0, comp_ref.shape[1] // WIDTH, body, both)
    edge = both[0:ROWS] + both[ROWS:]
    if EDGE < 128:
        edge = jnp.concatenate([edge, jnp.zeros((ROWS, 128 - EDGE), f32)], axis=1)
    lane = lax.broadcasted_iota(jnp.int32, (32, 128), 1)
    rest = pltpu.roll(jnp.concatenate([edge[32:], jnp.zeros((8, 128), f32)], axis=0), 64, 1)
    edge_ref[...] = jnp.where(lane < 64, edge[0:32], rest)


def main_kernel(comp_ref, mass_ref, cell_ref, les_ref, rate_ref, main_ref, cells_ref, w_ref):
    own_cells(les_ref, rate_ref, cells_ref)
    w = weighted(comp_ref, mass_ref, w_ref)
    band, index = band_and_index(*local_cells(cell_ref[...]))
    banded = [w * jnp.where(band == k, 1.0, 0.0).astype(bf16) for k in range(GROUPS)]
    both = dot_nt(jnp.concatenate(banded, axis=0), hot(index, 2 * CY))
    lane = lax.broadcasted_iota(jnp.int32, (ROWS, CY), 1)
    inner = (lane >= R) & (lane < CY - R)
    for k in range(GROUPS):
        start = 2 * ROWS * k
        sums = both[start : start + ROWS] + both[start + ROWS : start + 2 * ROWS]
        for odd in range(2):
            part = sums[:, odd * CY : (odd + 1) * CY]
            x = 2 * k + odd - R
            if 0 <= x < CX:
                part = part + jnp.where(inner, cells_ref[:, x * CY : (x + 1) * CY], 0.0)
            main_ref[k * ROWS : (k + 1) * ROWS, odd * CY : (odd + 1) * CY] = part


def pack_kernel(main_ref, edge_ref, even_in_ref, odd_in_ref, odd_ref, even_ref):
    odd_y = lax.axis_index("gy") % 2 == 1
    odd_x = lax.axis_index("gx") % 2 == 1
    even_in = even_in_ref[...]
    odd_in = odd_in_ref[...]
    row = lax.axis_index("gy")
    upper = jnp.where(row < lax.axis_size("gy") - 1, jnp.where(odd_y, odd_in, even_in), 0.0)
    lower = jnp.where(row > 0, jnp.where(odd_y, even_in, odd_in), 0.0)
    lane = lax.broadcasted_iota(jnp.int32, (32, 128), 1)
    high = (lane & 16) != 0
    both = edge_ref[...] + jnp.where(high, pltpu.roll(upper, 16, 1), pltpu.roll(lower, 112, 1))
    edge = jnp.concatenate([both, pltpu.roll(both, 64, 1)[0 : ROWS - 32]], axis=0)
    half = 2 * ROWS
    left, right = main_ref[0:half, :], main_ref[half:, :]
    even_ref[0:half, :] = jnp.where(odd_x, left, right)
    odd_ref[0:half, :] = jnp.where(odd_x, right, left)
    left_edge, right_edge = edge, pltpu.roll(edge, 96, 1)
    quarter = lane[0:8] >> 5
    for ref, part in (
        (even_ref, jnp.where(odd_x, left_edge, right_edge)),
        (odd_ref, jnp.where(odd_x, right_edge, left_edge)),
    ):
        for side in range(2):
            packed = jnp.zeros((8, 128), f32)
            for k in range(4):
                block = side * 4 + k
                if block < ROWS // 8:
                    rows = part[block * 8 : block * 8 + 8]
                    moved = pltpu.roll(rows, 32 * k, 1) if k else rows
                    packed = jnp.where(quarter == k, moved, packed)
            ref[half : half + 8, side * 128 : (side + 1) * 128] = packed


def table(total):
    rows = lax.broadcasted_iota(jnp.int32, total.shape, 0)
    mass = total[NSP : NSP + 1]
    mass = jnp.where(mass > 0.0, mass, 1.0)
    means = total / mass
    keep = jnp.exp(-total[NSP + 1 : NSP + 2])
    return means, jnp.where(rows < NSP, (1.0 - keep) * means, jnp.where(rows == NSP, keep, 0.0))


def unpacked(packed):
    lane = lax.broadcasted_iota(jnp.int32, (8, 128), 1)
    blocks = []
    for block in range(ROWS // 8):
        side, k = divmod(block, 4)
        rows = packed[:, side * 128 : (side + 1) * 128]
        rows = pltpu.roll(rows, 128 - 32 * k, 1) if k else rows
        blocks.append(jnp.where(lane < 32, rows, 0.0))
    return jnp.concatenate(blocks, axis=0)


def operator_rows(matrix_ref, full_ref, out_ref, scale):
    full_ref[...] = jnp.zeros_like(full_ref)
    start = 0
    for level, active in enumerate((NS_LOW, NS_MID, NSP)):
        rows = -(-active // 8) * 8
        count = min(rows, NSP)
        row = lax.broadcasted_iota(jnp.int32, (count, NSP), 0)
        col = lax.broadcasted_iota(jnp.int32, (count, NSP), 1)
        block = matrix_ref[level, 0:count, :] * scale
        high, low = split(jnp.where((row < active) & (col < active), block, 0.0))
        full_ref[start : start + count, 0:NSP] = high
        full_ref[start : start + count, 64 : 64 + NSP] = high
        full_ref[start : start + count, 128 : 128 + NSP] = low
        start += rows
    out_ref[...] = full_ref[...].astype(bf16)


def three(x):
    high = x.astype(bf16)
    low = (x - high.astype(f32)).astype(bf16)
    return jnp.concatenate([high, low, high], axis=0)


def prepare_kernel(cell_ref, level_ref, rate_ref, map_ref, hot_ref, which_ref, ops_ref, maps_ref, full_ref):
    operator_rows(rate_ref, full_ref, ops_ref, 1.0)
    operator_rows(map_ref, full_ref, maps_ref, chem_step)
    particles = cell_ref.shape[1]
    which_ref[1:2, :] = level_ref[...].reshape(1, particles)

    def body(i, carry):
        at = pl.ds(pl.multiple_of(i * CHUNK, CHUNK), CHUNK)
        band, index = band_and_index(*local_cells(cell_ref[:, at]))
        which_ref[0:1, at] = band
        index = jnp.concatenate([index, jnp.where(band == GROUPS, index + 64, index)], axis=0)
        hot_ref[:, at] = hot_pair(index, 2 * CY)
        return carry

    lax.fori_loop(0, particles // CHUNK, body, 0)


def react_kernel(
    odd_ref, even_ref, odd_in_ref, even_in_ref, ops_ref, maps_ref, hot_ref, which_ref, comp_ref,
    updated_hbm, means_hbm,
    means_ref, full_ref, cells_ref, mixed_ref, out_ref, sems,
):
    half = 2 * ROWS
    odd_x = lax.axis_index("gx") % 2 == 1
    even = even_ref[...] + even_in_ref[...]
    column = lax.axis_index("gx")
    at_end = (column == 0) | (column == lax.axis_size("gx") - 1)
    odd = odd_ref[...] + jnp.where(at_end, 0.0, odd_in_ref[...])
    left = jnp.where(odd_x, even, odd)
    right = jnp.where(odd_x, odd, even)
    edge = unpacked(left[half:, :]) + pltpu.roll(unpacked(right[half:, :]), 32, 1)
    lane = lax.broadcasted_iota(jnp.int32, (ROWS, 128), 1)
    edge_means, edge_table = table(edge)
    start = GROUPS * half
    full_ref[start:, 128:] = jnp.zeros((ROWS, 128), f32)
    high, low = split(edge_table)
    full_ref[start:, 0:128] = jnp.where(lane < 64, high, pltpu.roll(low, 64, 1))
    high, low = split(edge_means)
    edge_means = jnp.where(lane < 64, high, pltpu.roll(low, 64, 1)).astype(bf16)
    row = lax.broadcasted_iota(jnp.int32, (128, CY), 0) & 63
    col = lax.broadcasted_iota(jnp.int32, (1, CY), 1)
    inner = (lane >= R) & (lane < CY - R)
    for group in range(GROUPS):
        source = left if group < 2 else right
        start = (group % 2) * ROWS
        means, cells = table(source[start : start + ROWS])
        high, low = split(cells)
        full_ref[group * half : group * half + ROWS, :] = high
        full_ref[group * half + ROWS : (group + 1) * half, :] = low
        if group in (1, 2):
            for odd_column in range(2):
                x = group * 2 + odd_column - R
                index = edge_index(jnp.full((1, CY), x + R, jnp.int32), col + R)
                placed = dot(edge_means, jnp.where(row == index, 1.0, 0.0).astype(bf16))
                own = jnp.where(inner, means[:, odd_column * CY : (odd_column + 1) * CY], placed)
                means_ref[:, x, :] = own[0:NSP]
    means_copy = pltpu.make_async_copy(means_ref, means_hbm, sems.at[0])
    means_copy.start()
    cells_ref[...] = full_ref[...].astype(bf16)
    mixed_ref[...] = jnp.zeros_like(mixed_ref)
    chunks = len(CHUNKS)
    sent = []

    for chunk in range(chunks):
        width = CHUNKS[chunk]
        at = pl.ds(sum(CHUNKS[:chunk]), width)
        gathered = dot(cells_ref[...], hot_ref[:, at])
        band = which_ref[0:1, at]
        chosen = gathered[0:half]
        for k in range(1, GROUPS):
            chosen = jnp.where(band == k, gathered[k * half : (k + 1) * half], chosen)
        value = jnp.where(band == GROUPS, gathered[GROUPS * half :], chosen[0:ROWS] + chosen[ROWS:])
        mixed_ref[0:NSP, 0:width] = comp_ref[:, at] * value[NSP : NSP + 1] + value[0:NSP]
        level = which_ref[1:2, at]
        first, second = level == 0, level == 1
        z = dot(ops_ref[...], three(mixed_ref[:, 0:width]))
        z = jnp.concatenate(
            [jnp.where(first, z[0:24], jnp.where(second, z[24:48], z[48:72])), z[72:104]], axis=0
        )
        source = jnp.concatenate([jnp.tanh(z), jnp.zeros((8, width), f32)], axis=0)
        parts = three(source)
        begin = 0
        for stretch in STRETCHES[chunk]:
            inside = slice(begin, begin + stretch)
            z = dot(maps_ref[...], parts[:, inside])
            one, two = first[:, inside], second[:, inside]
            change = jnp.concatenate(
                [
                    jnp.where(one, z[0:24], jnp.where(two, z[24:48], z[48:72])),
                    jnp.where(level[:, inside] == 2, z[72:104], 0.0),
                ],
                axis=0,
            )
            columns = pl.ds(sum(CHUNKS[:chunk]) + begin, stretch)
            out_ref[:, columns] = mixed_ref[0:NSP, inside] + change[0:NSP]
            out = pltpu.make_async_copy(
                out_ref.at[:, columns], updated_hbm.at[:, columns], sems.at[1 + len(sent)]
            )
            out.start()
            sent.append(out)
            begin += stretch
    means_copy.wait()
    for out in sent:
        out.wait()


def swap(x, axis, odd):
    columns, rows = lax.axis_size("gx"), lax.axis_size("gy")

    def partner(i, j):
        at, count = (i, columns) if axis == "gx" else (j, rows)
        other = at + 1 if at % 2 == odd else at - 1
        if axis == "gx":
            return (other, j) if 0 <= other < count else (i, j ^ 1)
        return (i, other) if 0 <= other < count else (i ^ 1, j)

    pairs = []
    for i in range(columns):
        for j in range(rows):
            k, m = partner(i, j)
            pairs.append((i * rows + j, k * rows + m))
    return lax.ppermute(x, ("gx", "gy"), pairs)


def per_device(
    composition,
    particle_mass,
    particle_cell,
    particle_level,
    les_mean,
    mix_rate,
    rate_matrix,
    implicit_map,
):
    particles = composition.shape[1]
    sds = jax.ShapeDtypeStruct
    stay = lambda x: pltpu.with_memory_space_constraint(x, pltpu.HBM)
    hbm = pl.BlockSpec(memory_space=pltpu.HBM)
    vmem = pl.BlockSpec(memory_space=pltpu.VMEM)
    prior = pltpu.VMEM((ROWS, CX * CY), f32)
    edge, local, mass, cell, les, rate = pl.pallas_call(
        edge_kernel,
        out_shape=(
            sds((32, 128), f32),
            sds(composition.shape, f32),
            sds(particle_mass.shape, f32),
            sds(particle_cell.shape, jnp.int32),
            sds(les_mean.shape, f32),
            sds(mix_rate.shape, f32),
        ),
        in_specs=[hbm] * 5,
        out_specs=(vmem,) * 6,
        scratch_shapes=[
            prior,
            pltpu.VMEM((ROWS, WIDTH), f32),
            pltpu.SemaphoreType.DMA((4 + particles // WIDTH,)),
        ],
        compiler_params=VMEM,
        name="edge_sums",
    )(*map(stay, (composition, particle_mass, particle_cell, les_mean, mix_rate)))
    main = pl.pallas_call(
        main_kernel,
        out_shape=sds((GROUPS * ROWS, 2 * CY), f32),
        in_specs=[vmem] * 5,
        out_specs=vmem,
        scratch_shapes=[prior, pltpu.VMEM((ROWS, particles), f32)],
        compiler_params=VMEM,
        cost_estimate=pl.CostEstimate(flops=1 << 32, bytes_accessed=8 << 20, transcendentals=0),
        name="cell_sums",
    )(local, mass, cell, les, rate)
    edge_even = swap(edge, "gy", 0)
    edge_odd = swap(edge, "gy", 1)
    payload = sds((2 * ROWS + 8, 2 * CY), f32)
    odd, even = pl.pallas_call(
        pack_kernel,
        out_shape=(payload, payload),
        compiler_params=VMEM,
        name="pack",
    )(main, edge, edge_even, edge_odd)
    odd_in = swap(odd, "gx", 1)
    even_in = swap(even, "gx", 0)
    operator = sds((104, 192), bf16)
    places, which, ops, maps = pl.pallas_call(
        prepare_kernel,
        out_shape=(sds((2 * CY, particles), bf16), sds((2, particles), jnp.int32), operator, operator),
        in_specs=[vmem] * 4,
        out_specs=(vmem,) * 4,
        scratch_shapes=[pltpu.VMEM((104, 192), f32)],
        compiler_params=VMEM,
        cost_estimate=pl.CostEstimate(flops=1 << 22, bytes_accessed=8 << 20, transcendentals=0),
        name="prepare",
    )(cell, particle_level, rate_matrix, implicit_map)
    return pl.pallas_call(
        react_kernel,
        out_shape=(sds(composition.shape, f32), sds(les_mean.shape, f32)),
        in_specs=[vmem] * 9,
        out_specs=(hbm, hbm),
        scratch_shapes=[
            pltpu.VMEM(les_mean.shape, f32),
            pltpu.VMEM(((BANDS + GROUPS) * ROWS, 2 * CY), f32),
            pltpu.VMEM(((BANDS + GROUPS) * ROWS, 2 * CY), bf16),
            pltpu.VMEM((64, max(CHUNKS)), f32),
            pltpu.VMEM(composition.shape, f32),
            pltpu.SemaphoreType.DMA((sum(map(len, STRETCHES)) + 1,)),
        ],
        compiler_params=VMEM,
        name="gather_react",
    )(odd, even, odd_in, even_in, ops, maps, places, which, local)


def solution(mesh):
    placed = (
        P(None, ("gx", "gy")),
        P(("gx", "gy")),
        P(None, ("gx", "gy")),
        P(("gx", "gy")),
        P(None, "gx", "gy"),
        P("gx", "gy"),
        P(),
        P(),
    )
    return jax.shard_map(
        per_device,
        mesh=mesh,
        in_specs=placed,
        out_specs=(P(None, ("gx", "gy")), P(None, "gx", "gy")),
        check_vma=False,
    )
```

```python
import jax
import jax.numpy as jnp
from jax import lax
from jax.experimental import pallas as pl
from jax.experimental.pallas import tpu as pltpu
from jax.sharding import PartitionSpec as P

NS_LOW = 21
NS_MID = 24
NSP = 53
R = 2
CX = 4
CY = 128
ROWS = 56
GROUPS = 4
BANDS = GROUPS + 1
ROWBLOCK = 16
EDGE = 64
WIDTH = 4096
CHUNK = 4096
CHUNKS = (5120, 3072)
STRETCHES = ((5120,), (1536, 1536))
VMEM = pltpu.CompilerParams(vmem_limit_bytes=40 << 20)

prior_weight = 16.0
chem_step = 0.5

f32 = jnp.float32
bf16 = jnp.bfloat16


def split(x):
    high = x.astype(bf16).astype(f32)
    return high, x - high


def stacked(x):
    high, low = split(x)
    return jnp.concatenate([high, low], axis=0).astype(bf16)


def local_cells(cells):
    local_x = cells[0:1, :] - (lax.axis_index("gx") * CX - R)
    local_y = cells[1:2, :] - (lax.axis_index("gy") * CY - R)
    return local_x, local_y


def edge_index(local_x, local_y):
    place = jnp.where(local_y < 2 * R, local_y, local_y - CY + 16)
    return (local_x >> 2) * 32 + (local_x & 3) * 4 + place


def band_and_index(local_x, local_y):
    inside = (local_y >= 2 * R) & (local_y < CY)
    band = jnp.where(inside, local_x >> 1, GROUPS)
    index = jnp.where(inside, (local_x & 1) * CY + local_y - R, edge_index(local_x, local_y))
    return band, index


def hot(index, count):
    cells = lax.broadcasted_iota(jnp.int32, (count, index.shape[1]), 0)
    return jnp.where(cells == index, 1.0, 0.0).astype(bf16)


def hot_pair(index, count):
    cells = lax.broadcasted_iota(jnp.int32, (count, index.shape[1]), 0)
    return jnp.where((cells == index[0:1]) | (cells == index[1:2]), 1.0, 0.0).astype(bf16)


def dot_nt(a, b):
    return lax.dot_general(a, b, (((1,), (1,)), ((), ())), preferred_element_type=f32)


def dot(a, b):
    return jnp.dot(a, b, preferred_element_type=f32)


def own_cells(les_ref, rate_ref, cells_ref):
    cells_ref[NSP:, :] = jnp.zeros((ROWS - NSP, CX * CY), f32)
    for x in range(CX):
        at = slice(x * CY, (x + 1) * CY)
        cells_ref[0:NSP, at] = prior_weight * les_ref[:, x, :]
        cells_ref[NSP : NSP + 1, at] = jnp.full((1, CY), prior_weight, f32)
        cells_ref[NSP + 1 : NSP + 2, at] = rate_ref[x : x + 1, :]


def weighted(comp_ref, mass_ref, w_ref):
    particles = comp_ref.shape[1]
    mass = mass_ref[...].reshape(1, particles)
    w_ref[0:NSP, :] = comp_ref[...] * mass
    w_ref[NSP : NSP + 1, :] = mass
    w_ref[NSP + 1 :, :] = jnp.zeros((ROWS - NSP - 1, particles), f32)
    return stacked(w_ref[...])


def edge_kernel(
    comp_hbm, mass_hbm, cell_hbm, les_hbm, rate_hbm, edge_ref, comp_ref,
    mass_ref, cell_ref, les_ref, rate_ref, cells_ref, w_ref, sems,
):
    pairs = [(les_hbm, les_ref), (rate_hbm, rate_ref), (cell_hbm, cell_ref), (mass_hbm, mass_ref)]
    small = len(pairs)
    for start in range(0, comp_ref.shape[1], WIDTH):
        at = pl.ds(start, WIDTH)
        pairs.append((comp_hbm.at[:, at], comp_ref.at[:, at]))
    copies = [pltpu.make_async_copy(src, dst, sems.at[i]) for i, (src, dst) in enumerate(pairs)]
    for i in (0, 1, 4, 2, 3, *range(5, len(copies))):
        copies[i].start()
    cells = CX * CY
    cell = lax.broadcasted_iota(jnp.int32, (1, cells), 1)
    band, index = band_and_index(cell // CY + R, cell % CY + R)
    place = hot(jnp.where(band == GROUPS, index, -1), EDGE)
    copies[0].wait()
    copies[1].wait()
    own_cells(les_ref, rate_ref, cells_ref)
    both = dot_nt(stacked(cells_ref[...]), place)
    for copy in copies[2:small]:
        copy.wait()
    w_ref[NSP + 1 :, :] = jnp.zeros((ROWS - NSP - 1, WIDTH), f32)

    def body(i, total):
        at = pl.ds(pl.multiple_of(i * WIDTH, WIDTH), WIDTH)
        pltpu.make_async_copy(comp_hbm.at[:, at], comp_ref.at[:, at], sems.at[small + i]).wait()
        mass = mass_ref[at].reshape(1, WIDTH)
        w_ref[0:NSP, :] = comp_ref[:, at] * mass
        w_ref[NSP : NSP + 1, :] = mass
        band, index = band_and_index(*local_cells(cell_ref[:, at]))
        place = hot(jnp.where(band == GROUPS, index, -1), EDGE)
        return total + dot_nt(stacked(w_ref[...]), place)

    both = lax.fori_loop(0, comp_ref.shape[1] // WIDTH, body, both)
    edge = both[0:ROWS] + both[ROWS:]
    if EDGE < 128:
        edge = jnp.concatenate([edge, jnp.zeros((ROWS, 128 - EDGE), f32)], axis=1)
    lane = lax.broadcasted_iota(jnp.int32, (32, 128), 1)
    rest = pltpu.roll(jnp.concatenate([edge[32:], jnp.zeros((8, 128), f32)], axis=0), 64, 1)
    edge_ref[...] = jnp.where(lane < 64, edge[0:32], rest)


def main_kernel(comp_ref, mass_ref, cell_ref, les_ref, rate_ref, main_ref, cells_ref, w_ref):
    own_cells(les_ref, rate_ref, cells_ref)
    w = weighted(comp_ref, mass_ref, w_ref)
    band, index = band_and_index(*local_cells(cell_ref[...]))
    banded = [w * jnp.where(band == k, 1.0, 0.0).astype(bf16) for k in range(GROUPS)]
    both = dot_nt(jnp.concatenate(banded, axis=0), hot(index, 2 * CY))
    lane = lax.broadcasted_iota(jnp.int32, (ROWS, CY), 1)
    inner = (lane >= R) & (lane < CY - R)
    for k in range(GROUPS):
        start = 2 * ROWS * k
        sums = both[start : start + ROWS] + both[start + ROWS : start + 2 * ROWS]
        for odd in range(2):
            part = sums[:, odd * CY : (odd + 1) * CY]
            x = 2 * k + odd - R
            if 0 <= x < CX:
                part = part + jnp.where(inner, cells_ref[:, x * CY : (x + 1) * CY], 0.0)
            main_ref[k * ROWS : (k + 1) * ROWS, odd * CY : (odd + 1) * CY] = part


def pack_kernel(main_ref, edge_ref, even_in_ref, odd_in_ref, odd_ref, even_ref):
    odd_y = lax.axis_index("gy") % 2 == 1
    odd_x = lax.axis_index("gx") % 2 == 1
    even_in = even_in_ref[...]
    odd_in = odd_in_ref[...]
    row = lax.axis_index("gy")
    upper = jnp.where(row < lax.axis_size("gy") - 1, jnp.where(odd_y, odd_in, even_in), 0.0)
    lower = jnp.where(row > 0, jnp.where(odd_y, even_in, odd_in), 0.0)
    lane = lax.broadcasted_iota(jnp.int32, (32, 128), 1)
    high = (lane & 16) != 0
    both = edge_ref[...] + jnp.where(high, pltpu.roll(upper, 16, 1), pltpu.roll(lower, 112, 1))
    edge = jnp.concatenate([both, pltpu.roll(both, 64, 1)[0 : ROWS - 32]], axis=0)
    half = 2 * ROWS
    left, right = main_ref[0:half, :], main_ref[half:, :]
    even_ref[0:half, :] = jnp.where(odd_x, left, right)
    odd_ref[0:half, :] = jnp.where(odd_x, right, left)
    left_edge, right_edge = edge, pltpu.roll(edge, 96, 1)
    quarter = lane[0:8] >> 5
    for ref, part in (
        (even_ref, jnp.where(odd_x, left_edge, right_edge)),
        (odd_ref, jnp.where(odd_x, right_edge, left_edge)),
    ):
        for side in range(2):
            packed = jnp.zeros((8, 128), f32)
            for k in range(4):
                block = side * 4 + k
                if block < ROWS // 8:
                    rows = part[block * 8 : block * 8 + 8]
                    moved = pltpu.roll(rows, 32 * k, 1) if k else rows
                    packed = jnp.where(quarter == k, moved, packed)
            ref[half : half + 8, side * 128 : (side + 1) * 128] = packed


def table(total):
    rows = lax.broadcasted_iota(jnp.int32, total.shape, 0)
    mass = total[NSP : NSP + 1]
    mass = jnp.where(mass > 0.0, mass, 1.0)
    means = total / mass
    keep = jnp.exp(-total[NSP + 1 : NSP + 2])
    return means, jnp.where(rows < NSP, (1.0 - keep) * means, jnp.where(rows == NSP, keep, 0.0))


def unpacked(packed):
    lane = lax.broadcasted_iota(jnp.int32, (8, 128), 1)
    blocks = []
    for block in range(ROWS // 8):
        side, k = divmod(block, 4)
        rows = packed[:, side * 128 : (side + 1) * 128]
        rows = pltpu.roll(rows, 128 - 32 * k, 1) if k else rows
        blocks.append(jnp.where(lane < 32, rows, 0.0))
    return jnp.concatenate(blocks, axis=0)


def operator_rows(matrix_ref, full_ref, out_ref, scale):
    full_ref[...] = jnp.zeros_like(full_ref)
    start = 0
    for level, active in enumerate((NS_LOW, NS_MID, NSP)):
        rows = -(-active // 8) * 8
        count = min(rows, NSP)
        row = lax.broadcasted_iota(jnp.int32, (count, NSP), 0)
        col = lax.broadcasted_iota(jnp.int32, (count, NSP), 1)
        block = matrix_ref[level, 0:count, :] * scale
        high, low = split(jnp.where((row < active) & (col < active), block, 0.0))
        full_ref[start : start + count, 0:NSP] = high
        full_ref[start : start + count, 64 : 64 + NSP] = high
        full_ref[start : start + count, 128 : 128 + NSP] = low
        start += rows
    out_ref[...] = full_ref[...].astype(bf16)


def three(x):
    high = x.astype(bf16)
    low = (x - high.astype(f32)).astype(bf16)
    return jnp.concatenate([high, low, high], axis=0)


def prepare_kernel(cell_ref, level_ref, rate_ref, map_ref, hot_ref, which_ref, ops_ref, maps_ref, full_ref):
    operator_rows(rate_ref, full_ref, ops_ref, 1.0)
    operator_rows(map_ref, full_ref, maps_ref, chem_step)
    particles = cell_ref.shape[1]
    which_ref[1:2, :] = level_ref[...].reshape(1, particles)

    def body(i, carry):
        at = pl.ds(pl.multiple_of(i * CHUNK, CHUNK), CHUNK)
        band, index = band_and_index(*local_cells(cell_ref[:, at]))
        which_ref[0:1, at] = band
        index = jnp.concatenate([index, jnp.where(band == GROUPS, index + 64, index)], axis=0)
        hot_ref[:, at] = hot_pair(index, 2 * CY)
        return carry

    lax.fori_loop(0, particles // CHUNK, body, 0)


def react_kernel(
    odd_ref, even_ref, odd_in_ref, even_in_ref, ops_ref, maps_ref, hot_ref, which_ref, comp_ref,
    updated_hbm, means_hbm,
    means_ref, full_ref, cells_ref, mixed_ref, out_ref, sems,
):
    half = 2 * ROWS
    odd_x = lax.axis_index("gx") % 2 == 1
    even = even_ref[...] + even_in_ref[...]
    column = lax.axis_index("gx")
    at_end = (column == 0) | (column == lax.axis_size("gx") - 1)
    odd = odd_ref[...] + jnp.where(at_end, 0.0, odd_in_ref[...])
    left = jnp.where(odd_x, even, odd)
    right = jnp.where(odd_x, odd, even)
    edge = unpacked(left[half:, :]) + pltpu.roll(unpacked(right[half:, :]), 32, 1)
    lane = lax.broadcasted_iota(jnp.int32, (ROWS, 128), 1)
    edge_means, edge_table = table(edge)
    start = GROUPS * half
    full_ref[start:, 128:] = jnp.zeros((ROWS, 128), f32)
    high, low = split(edge_table)
    full_ref[start:, 0:128] = jnp.where(lane < 64, high, pltpu.roll(low, 64, 1))
    high, low = split(edge_means)
    edge_means = jnp.where(lane < 64, high, pltpu.roll(low, 64, 1)).astype(bf16)
    row = lax.broadcasted_iota(jnp.int32, (128, CY), 0) & 63
    col = lax.broadcasted_iota(jnp.int32, (1, CY), 1)
    inner = (lane >= R) & (lane < CY - R)
    for group in range(GROUPS):
        source = left if group < 2 else right
        start = (group % 2) * ROWS
        means, cells = table(source[start : start + ROWS])
        high, low = split(cells)
        full_ref[group * half : group * half + ROWS, :] = high
        full_ref[group * half + ROWS : (group + 1) * half, :] = low
        if group in (1, 2):
            for odd_column in range(2):
                x = group * 2 + odd_column - R
                index = edge_index(jnp.full((1, CY), x + R, jnp.int32), col + R)
                placed = dot(edge_means, jnp.where(row == index, 1.0, 0.0).astype(bf16))
                own = jnp.where(inner, means[:, odd_column * CY : (odd_column + 1) * CY], placed)
                means_ref[:, x, :] = own[0:NSP]
    means_copy = pltpu.make_async_copy(means_ref, means_hbm, sems.at[0])
    means_copy.start()
    cells_ref[...] = full_ref[...].astype(bf16)
    mixed_ref[...] = jnp.zeros_like(mixed_ref)
    chunks = len(CHUNKS)
    sent = []

    for chunk in range(chunks):
        width = CHUNKS[chunk]
        at = pl.ds(sum(CHUNKS[:chunk]), width)
        gathered = dot(cells_ref[...], hot_ref[:, at])
        band = which_ref[0:1, at]
        chosen = gathered[0:half]
        for k in range(1, GROUPS):
            chosen = jnp.where(band == k, gathered[k * half : (k + 1) * half], chosen)
        value = jnp.where(band == GROUPS, gathered[GROUPS * half :], chosen[0:ROWS] + chosen[ROWS:])
        mixed_ref[0:NSP, 0:width] = comp_ref[:, at] * value[NSP : NSP + 1] + value[0:NSP]
        level = which_ref[1:2, at]
        first, second = level == 0, level == 1
        z = dot(ops_ref[...], three(mixed_ref[:, 0:width]))
        z = jnp.concatenate(
            [jnp.where(first, z[0:24], jnp.where(second, z[24:48], z[48:72])), z[72:104]], axis=0
        )
        source = jnp.concatenate([jnp.tanh(z), jnp.zeros((8, width), f32)], axis=0)
        parts = three(source)
        begin = 0
        for stretch in STRETCHES[chunk]:
            inside = slice(begin, begin + stretch)
            z = dot(maps_ref[...], parts[:, inside])
            one, two = first[:, inside], second[:, inside]
            change = jnp.concatenate(
                [
                    jnp.where(one, z[0:24], jnp.where(two, z[24:48], z[48:72])),
                    jnp.where(level[:, inside] == 2, z[72:104], 0.0),
                ],
                axis=0,
            )
            columns = pl.ds(sum(CHUNKS[:chunk]) + begin, stretch)
            out_ref[:, columns] = mixed_ref[0:NSP, inside] + change[0:NSP]
            out = pltpu.make_async_copy(
                out_ref.at[:, columns], updated_hbm.at[:, columns], sems.at[1 + len(sent)]
            )
            out.start()
            sent.append(out)
            begin += stretch
    means_copy.wait()
    for out in sent:
        out.wait()


def swap(x, axis, odd):
    columns, rows = lax.axis_size("gx"), lax.axis_size("gy")

    def partner(i, j):
        at, count = (i, columns) if axis == "gx" else (j, rows)
        other = at + 1 if at % 2 == odd else at - 1
        if axis == "gx":
            return (other, j) if 0 <= other < count else (i, j ^ 1)
        return (i, other) if 0 <= other < count else (i ^ 1, j)

    pairs = []
    for i in range(columns):
        for j in range(rows):
            k, m = partner(i, j)
            pairs.append((i * rows + j, k * rows + m))
    return lax.ppermute(x, ("gx", "gy"), pairs)


def per_device(
    composition,
    particle_mass,
    particle_cell,
    particle_level,
    les_mean,
    mix_rate,
    rate_matrix,
    implicit_map,
):
    particles = composition.shape[1]
    sds = jax.ShapeDtypeStruct
    stay = lambda x: pltpu.with_memory_space_constraint(x, pltpu.HBM)
    hbm = pl.BlockSpec(memory_space=pltpu.HBM)
    vmem = pl.BlockSpec(memory_space=pltpu.VMEM)
    prior = pltpu.VMEM((ROWS, CX * CY), f32)
    edge, local, mass, cell, les, rate = pl.pallas_call(
        edge_kernel,
        out_shape=(
            sds((32, 128), f32),
            sds(composition.shape, f32),
            sds(particle_mass.shape, f32),
            sds(particle_cell.shape, jnp.int32),
            sds(les_mean.shape, f32),
            sds(mix_rate.shape, f32),
        ),
        in_specs=[hbm] * 5,
        out_specs=(vmem,) * 6,
        scratch_shapes=[
            prior,
            pltpu.VMEM((ROWS, WIDTH), f32),
            pltpu.SemaphoreType.DMA((4 + particles // WIDTH,)),
        ],
        compiler_params=VMEM,
        name="edge_sums",
    )(*map(stay, (composition, particle_mass, particle_cell, les_mean, mix_rate)))
    main = pl.pallas_call(
        main_kernel,
        out_shape=sds((GROUPS * ROWS, 2 * CY), f32),
        in_specs=[vmem] * 5,
        out_specs=vmem,
        scratch_shapes=[prior, pltpu.VMEM((ROWS, particles), f32)],
        compiler_params=VMEM,
        cost_estimate=pl.CostEstimate(flops=1 << 32, bytes_accessed=8 << 20, transcendentals=0),
        name="cell_sums",
    )(local, mass, cell, les, rate)
    edge_even = swap(edge, "gy", 0)
    edge_odd = swap(edge, "gy", 1)
    payload = sds((2 * ROWS + 8, 2 * CY), f32)
    odd, even = pl.pallas_call(
        pack_kernel,
        out_shape=(payload, payload),
        compiler_params=VMEM,
        name="pack",
    )(main, edge, edge_even, edge_odd)
    odd_in = swap(odd, "gx", 1)
    even_in = swap(even, "gx", 0)
    operator = sds((104, 192), bf16)
    places, which, ops, maps = pl.pallas_call(
        prepare_kernel,
        out_shape=(sds((2 * CY, particles), bf16), sds((2, particles), jnp.int32), operator, operator),
        in_specs=[vmem] * 4,
        out_specs=(vmem,) * 4,
        scratch_shapes=[pltpu.VMEM((104, 192), f32)],
        compiler_params=VMEM,
        cost_estimate=pl.CostEstimate(flops=1 << 22, bytes_accessed=8 << 20, transcendentals=0),
        name="prepare",
    )(cell, particle_level, rate_matrix, implicit_map)
    return pl.pallas_call(
        react_kernel,
        out_shape=(sds(composition.shape, f32), sds(les_mean.shape, f32)),
        in_specs=[vmem] * 9,
        out_specs=(hbm, hbm),
        scratch_shapes=[
            pltpu.VMEM(les_mean.shape, f32),
            pltpu.VMEM(((BANDS + GROUPS) * ROWS, 2 * CY), f32),
            pltpu.VMEM(((BANDS + GROUPS) * ROWS, 2 * CY), bf16),
            pltpu.VMEM((64, max(CHUNKS)), f32),
            pltpu.VMEM(composition.shape, f32),
            pltpu.SemaphoreType.DMA((sum(map(len, STRETCHES)) + 1,)),
        ],
        compiler_params=VMEM,
        name="gather_react",
    )(odd, even, odd_in, even_in, ops, maps, places, which, local)


def solution(mesh):
    placed = (
        P(None, ("gx", "gy")),
        P(("gx", "gy")),
        P(None, ("gx", "gy")),
        P(("gx", "gy")),
        P(None, "gx", "gy"),
        P("gx", "gy"),
        P(),
        P(),
    )
    return jax.shard_map(
        per_device,
        mesh=mesh,
        in_specs=placed,
        out_specs=(P(None, ("gx", "gy")), P(None, "gx", "gy")),
        check_vma=False,
    )
```
